32 devices in a mesh: groups: 2 (over y), seq: 8 (over z, x), head: 2 (over core).
Axes of the slice: x: 2, y: 2, z: 4, core: 2. Of those that a mesh axis runs over, the one named last changes fastest.
Arguments:
- mixer_input: bfloat16 [2048, 8192], P(('groups', 'seq'), 'head'), parts along dimension 0, may hold values from -6 to 6
- keys_queries: bfloat16 [2048, 2, 512], P(('groups', 'seq'), None, 'head'), parts along dimension 0, may hold values from -6 to 6
- gate_input: bfloat16 [2048, 8192], P(('groups', 'seq'), 'head'), parts along dimension 0, may hold values from -6 to 6
- step_raw: bfloat16 [2048, 128], P(('groups', 'seq'), 'head'), parts along dimension 0, may hold values from -4 to 4
- mixer_weight: bfloat16 [4, 8192], P(None, 'head'), may hold values from -3 to 3
- mixer_bias: bfloat16 [8192], P('head'), may hold values from -3 to 3
- keyquery_weight: bfloat16 [4, 2, 512], P(None, None, 'head'), may hold values from -3 to 3
- keyquery_bias: bfloat16 [2, 512], P(None, 'head'), may hold values from -3 to 3
- step_bias: float32 [128], P('head'), may hold values from -4 to -1
- decay_log: float32 [128], P('head'), may hold values from -14 to 0
- skip_gain: float32 [128], P('head'), may hold values from 0.5 to 2
- norm_gain: float32 [8192], P('head'), may hold values from 0.25 to 1.75
- resets: int32 [16], P(('groups', 'seq')), parts along dimension 0, may hold values from 0 to 1, as said below
Outputs:
- mixed: bfloat16 [2048, 8192], P(('groups', 'seq'), 'head'), parts along dimension 0
The draws below stay inside these ranges and needn't reach their ends.
There are 2 independent parts, one for each index of `groups`. The reference program is written for one: setup_inputs(seed, part) draws one part's arguments, and reference() takes and returns one part's arrays. A program takes and returns all parts, laid end to end along the dimension named above; an argument that names none is the same for every part. Nothing has to cross between parts.
Inputs may be any that keep to these rules, and one draw needn't show every extreme that they name: resets[c] = 1 marks a document that starts at the first token of span c; some span after the first holds a 1.
All inputs are finite; a program needn't handle non-finite values.
Results may differ from the reference program's by a relative error of at most 0.0044.
The reference program's roundings to bfloat16 on the way (of `weight`) count: a program that leaves them out, or rounds other values in their place, can miss the bound.
Values may be sent and summed in bfloat16 or wider, within the bound.
A program may use at most 64 MiB of HBM per device.

```python
import math
import jax
import jax.numpy as jnp
from jax import lax

HEAD_SIZE = 64
STATE = 128
SPAN = 128
KERNEL = 4
HEADS = 128
GROUPS = 4
TOKENS = 1024
SPANS = 8


def draw_decay_log(key, part):
    key = jax.random.fold_in(key, 11)
    first_key, second_key, third_key = jax.random.split(key, 3)
    quick_heads = jax.random.randint(first_key, (HEADS,), 0, 2) == 0
    quick_log = jax.random.uniform(second_key, (HEADS,), jnp.float32, math.log(0.1), 0.0)
    slow_log = jax.random.uniform(third_key, (HEADS,), jnp.float32, math.log(0.3), math.log(3.0)) - math.log(TOKENS)
    return jnp.where(quick_heads, quick_log, slow_log).astype(jnp.float32)


def draw_resets(key, part):
    key = jax.random.fold_in(key, 23)
    first_key, second_key = jax.random.split(key, 2)
    reset_flags = (jax.random.randint(first_key, (SPANS,), 0, 32) == 0).astype(jnp.int32)
    forced = jax.random.randint(second_key, (), 1, SPANS)
    return jnp.where(jnp.arange(SPANS) == forced, 1, reset_flags).astype(jnp.int32)


def steps_of(stream_key, dims, cuts, low, largest):
    def one(position, blocks):
        steps = jax.random.uniform(jax.random.fold_in(jax.random.fold_in(stream_key, 6), position), (blocks,), jnp.float32, low / len(cuts), largest / len(cuts))
        return jnp.repeat(jnp.exp(steps), dims[position] // blocks).reshape((-1,) + (1,) * (len(dims) - position - 1))

    factor_of = one(*cuts[0])
    for cut in cuts[1:]:
        factor_of = factor_of * one(*cut)
    return factor_of


def gaussian(own_key, dims, deviation, most, shards=(), dtype=jnp.bfloat16):
    drawn = deviation * jax.random.normal(own_key, dims, jnp.float32)
    if shards:
        drawn = drawn * steps_of(own_key, dims, shards, -0.22, 0.18)
    return jnp.clip(drawn, -most, most).astype(dtype)


def setup_inputs(seed: int = 0, part: int = 0) -> dict:
    splits = jax.random.split(jax.random.key(seed), 14)
    own_keys = jax.random.split(jax.random.fold_in(splits[13], part), 14)
    mixer_input = gaussian(own_keys[0], (TOKENS, HEADS * HEAD_SIZE), 1.0, 6.0, ((0, 8), (1, 2)))
    keys_queries = gaussian(own_keys[1], (TOKENS, 2, GROUPS * STATE), 1.0, 6.0, ((0, 8), (2, 2)))
    gate_input = gaussian(own_keys[2], (TOKENS, HEADS * HEAD_SIZE), 1.0, 6.0, ((0, 8), (1, 2)))
    step_raw = gaussian(own_keys[3], (TOKENS, HEADS), 1.0, 4.0, ((0, 8), (1, 2)))
    mixer_weight = gaussian(splits[4], (KERNEL, HEADS * HEAD_SIZE), KERNEL ** -0.5, 3.0, ((1, 2),))
    mixer_bias = gaussian(splits[5], (HEADS * HEAD_SIZE,), 1.0, 3.0, ((0, 2),))
    keyquery_weight = gaussian(splits[6], (KERNEL, 2, GROUPS * STATE), KERNEL ** -0.5, 3.0, ((2, 2),))
    keyquery_bias = gaussian(splits[7], (2, GROUPS * STATE), 1.0, 3.0, ((1, 2),))
    step_bias = jnp.clip(-4.0 + 3.0 * jax.random.uniform(splits[8], (HEADS,), jnp.float32) ** steps_of(splits[8], (HEADS,), ((0, 2),), -0.2, 0.2), -4.0, -1.0)
    decay_log = draw_decay_log(jax.random.fold_in(splits[13], 71), part)
    skip_gain = jnp.clip(0.5 + 1.5 * jax.random.uniform(splits[10], (HEADS,), jnp.float32) ** steps_of(splits[10], (HEADS,), ((0, 2),), -0.2, 0.2), 0.5, 2.0)
    norm_gain = jnp.clip(1.0 + 0.15 * jax.random.normal(splits[11], (HEADS * HEAD_SIZE,), jnp.float32), 0.25, 1.75)
    resets = draw_resets(jax.random.fold_in(jax.random.fold_in(splits[13], part), 71), part)
    return dict(mixer_input=mixer_input, keys_queries=keys_queries, gate_input=gate_input, step_raw=step_raw, mixer_weight=mixer_weight, mixer_bias=mixer_bias, keyquery_weight=keyquery_weight, keyquery_bias=keyquery_bias, step_bias=step_bias, decay_log=decay_log, skip_gain=skip_gain, norm_gain=norm_gain, resets=resets)


def convolve(rim_block, raw_rows, weight, bias_row, survive):
    extended = jnp.concatenate([rim_block.astype(jnp.float32) * survive, raw_rows.astype(jnp.float32)], axis=0)
    running = jnp.broadcast_to(bias_row.astype(jnp.float32), raw_rows.shape)
    for tap_index in range(KERNEL):
        running = running + weight[tap_index].astype(jnp.float32) * extended[tap_index:tap_index + SPAN]
    return jax.nn.silu(running).astype(jnp.bfloat16)

def reference(mixer_input, keys_queries, gate_input, step_raw, mixer_weight, mixer_bias, keyquery_weight, keyquery_bias, step_bias, decay_log, skip_gain, norm_gain, resets):
    rim_count = KERNEL - 1
    heads_group = HEADS // GROUPS
    span_count = TOKENS // SPAN
    causal = jnp.arange(SPAN)[:, None] >= jnp.arange(SPAN)[None, :]

    def advance(carry, pieces):
        state_sum, rim_mixer, rim_pair = carry
        raw_mixer, raw_pair, gate_rows, raw_steps, reset_flag = pieces
        survive = (1 - reset_flag).astype(jnp.float32)
        value_rows = convolve(rim_mixer, raw_mixer, mixer_weight, mixer_bias, survive).reshape(SPAN, HEADS, HEAD_SIZE)
        pair_rows = convolve(rim_pair, raw_pair, keyquery_weight, keyquery_bias, survive)
        key_rows = pair_rows[:, 0].reshape(SPAN, GROUPS, STATE)
        query_rows = pair_rows[:, 1].reshape(SPAN, GROUPS, STATE)
        step_size = jax.nn.softplus(raw_steps.astype(jnp.float32) + step_bias)
        cumulative = jnp.cumsum(-jnp.exp(decay_log) * step_size, axis=0)
        scores = jnp.einsum('qgn,ugn->gqu', query_rows.astype(jnp.float32), key_rows.astype(jnp.float32))
        head_cum = cumulative.T
        log_gaps = head_cum[:, :, None] - head_cum[:, None, :]
        decays = jnp.exp(jnp.where(causal, log_gaps, -jnp.inf)).reshape(GROUPS, heads_group, SPAN, SPAN)
        step_cols = step_size.T.reshape(GROUPS, heads_group, 1, SPAN)
        mixing = (scores[:, None] * decays * step_cols).astype(jnp.bfloat16).reshape(HEADS, SPAN, SPAN)
        inside = jnp.einsum('hqu,uhp->qhp', mixing.astype(jnp.float32), value_rows.astype(jnp.float32))
        span_end = cumulative[-1]
        weighted = (jnp.exp(span_end[None, :] - cumulative)[:, :, None] * step_size[:, :, None] * value_rows.astype(jnp.float32)).astype(jnp.bfloat16)
        states = jnp.einsum('ugkp,ugn->gkpn', weighted.reshape(SPAN, GROUPS, heads_group, HEAD_SIZE).astype(jnp.float32), key_rows.astype(jnp.float32)).reshape(HEADS, HEAD_SIZE, STATE)
        entering = survive * state_sum
        read_back = jnp.einsum('qgn,gkpn->qgkp', query_rows.astype(jnp.float32), entering.reshape(GROUPS, heads_group, HEAD_SIZE, STATE), precision=lax.Precision.HIGHEST).reshape(SPAN, HEADS, HEAD_SIZE)
        result = inside + jnp.exp(cumulative)[:, :, None] * read_back + skip_gain[None, :, None] * value_rows.astype(jnp.float32)
        gated = result.reshape(SPAN, HEADS * HEAD_SIZE) * jax.nn.silu(gate_rows.astype(jnp.float32))
        grouped = gated.reshape(SPAN, GROUPS, -1)
        mean_square = lax.optimization_barrier(jnp.mean(grouped * grouped, axis=-1, keepdims=True))
        normed = (grouped * lax.rsqrt(mean_square + 1e-05)).reshape(SPAN, HEADS * HEAD_SIZE) * norm_gain
        next_state = jnp.exp(span_end)[:, None, None] * entering + states
        return ((next_state, raw_mixer[SPAN - rim_count:], raw_pair[SPAN - rim_count:]), normed.astype(jnp.bfloat16))
    initial = (jnp.zeros((HEADS, HEAD_SIZE, STATE), jnp.float32), jnp.zeros((rim_count, HEADS * HEAD_SIZE), jnp.bfloat16), jnp.zeros((rim_count, 2, GROUPS * STATE), jnp.bfloat16))
    sequence = (mixer_input.reshape(span_count, SPAN, -1), keys_queries.reshape(span_count, SPAN, 2, -1), gate_input.reshape(span_count, SPAN, -1), step_raw.reshape(span_count, SPAN, -1), resets)
    _, outputs = lax.scan(advance, initial, sequence)
    return outputs.reshape(TOKENS, HEADS * HEAD_SIZE)
```

```python
import functools

import jax
import jax.numpy as jnp
from jax import lax
from jax.experimental import pallas as pl
from jax.experimental.pallas import tpu as pltpu
from jax.sharding import PartitionSpec as P

HEAD_DEV = 64
GRP_DEV = 2
HEAD_SIZE = 64
STATE = 128
SPAN = 128
KERNEL = 4
RIM = KERNEL - 1
TILE = 256
TILE_HEADS = TILE // HEAD_SIZE
LOG2E = 1.4426950408889634
F32 = jnp.float32
BF16 = jnp.bfloat16
MESH = pl.DeviceIdType.MESH


def silu(x):
    half = 0.5 * x
    return half * jnp.tanh(half) + half


def two_terms(x):
    lane = lax.broadcasted_iota(jnp.int32, x.shape, 1)
    lead = x.astype(BF16).astype(F32)
    return jnp.where(lane < HEAD_DEV, lead, x - lead).astype(BF16)


def dot(a, b):
    return jnp.dot(a, b, preferred_element_type=F32)


def kernel(
    peers, tiles, split,
    x_ref, kq_ref, gate_ref, step_ref, wx_ref, bx_ref, wkq_ref, bkq_ref,
    sbias_ref, dlog_ref, skip_ref, gain_ref, resets_ref,
    out_ref,
    halo_send, halo_recv, halo, xs, kqs, vals, hot, w2, g2, cum2, row_t, keys_t, queries, scores, mask,
    rows2, f_send, f_recv, s_send, s_recv, s_own, c_recv, c_send, e_send, e_recv, e_own, res, mix_gate, ssq,
    one_send, one_recv, s_ssem, s_rsem, c_ssem, c_rsem, e_ssem, e_rsem,
):
    me = lax.axis_index("seq")
    side = lax.rem(me, 2)
    row = me // 2
    partner = me + 1 - 2 * side
    last_row = peers // 2 - 1
    features = tiles * TILE
    half_tiles = tiles // 2
    quarter = split

    barrier = pltpu.get_barrier_semaphore()
    for away in (-2, -1, 1, 2):
        @pl.when((me + away >= 0) & (me + away < peers))
        def _(away=away):
            pl.semaphore_signal(barrier, inc=1, device_id={"seq": me + away}, device_id_type=MESH)
    rim = jnp.concatenate(
        [x_ref[SPAN - 16 :, :].astype(F32)[16 - RIM :], kq_ref[SPAN - 16 :, :].astype(F32)[16 - RIM :]], axis=1
    )
    rim_parts = [rim[:, q * quarter : (q + 1) * quarter] for q in range(4)]
    halo_send[...] = jnp.concatenate(rim_parts + [jnp.zeros((4, quarter), F32)], axis=0).astype(BF16)
    pl.semaphore_wait(barrier, jnp.minimum(me, 2) + jnp.minimum(peers - 1 - me, 2))

    def remote(src, dst, ssem, rsem, target):
        return pltpu.make_async_remote_copy(
            src_ref=src, dst_ref=dst, send_sem=ssem, recv_sem=rsem, device_id={"seq": target}, device_id_type=MESH
        )

    halo_copy = remote(halo_send, halo_recv, one_send.at[0], one_recv.at[0], jnp.minimum(me + 1, peers - 1))

    @pl.when(me < peers - 1)
    def _():
        halo_copy.start()

    @pl.when(me == 0)
    def _():
        halo_recv[...] = jnp.zeros_like(halo_recv)

    survive = 1.0 - resets_ref[0].astype(F32)

    raw = step_ref[...].astype(F32)
    both = jnp.concatenate([raw, raw], axis=1)
    sbias = sbias_ref[...]
    dlog = dlog_ref[...]
    skip = skip_ref[...]
    logit = both + jnp.concatenate([sbias, sbias], axis=1)
    step = jnp.maximum(logit, 0.0) + jnp.log1p(jnp.exp(-jnp.abs(logit)))
    rate = (-LOG2E * jnp.exp(jnp.concatenate([dlog, dlog], axis=1))) * step
    t_idx = lax.broadcasted_iota(jnp.int32, (SPAN, SPAN), 0)
    s_idx = lax.broadcasted_iota(jnp.int32, (SPAN, SPAN), 1)
    lower = (t_idx >= s_idx).astype(F32)
    cum = jnp.dot(lower, rate, precision=lax.Precision.HIGHEST, preferred_element_type=F32)
    cum2[...] = cum
    end = cum[SPAN - 1 :, :]
    w2[...] = two_terms(jnp.exp2(end - cum) * step)
    g2[...] = two_terms(jnp.exp2(cum) * survive)
    factor = jnp.exp2(end) * survive
    f_send[...] = jnp.broadcast_to(factor, f_send.shape)
    f_copy = remote(f_send, f_recv, one_send.at[1], one_recv.at[1], partner)
    f_copy.start()
    row_t[...] = jnp.transpose(cum - jnp.log2(step))
    mask[...] = jnp.where(t_idx >= s_idx, 0.0, -1e30)

    @pl.loop(0, tiles)
    def _(t):
        r = lax.broadcasted_iota(jnp.int32, (SPAN, TILE), 0)
        c = lax.broadcasted_iota(jnp.int32, (SPAN, TILE), 1)
        hot[:, pl.ds(pl.multiple_of(t * TILE, TILE), TILE)] = (
            ((r & (HEAD_DEV - 1)) == t * TILE_HEADS + (c >> 6)).astype(F32).astype(BF16)
        )

    @pl.when(row == 0)
    def _():
        @pl.loop(0, half_tiles)
        def _(k):
            c_recv[k] = jnp.zeros((STATE, TILE), BF16)

    @pl.when(me > 0)
    def _():
        halo_copy.wait_recv()

    arrived = halo_recv[...].astype(F32) * survive
    for q in range(4):
        halo[8 - RIM :, q * quarter : (q + 1) * quarter] = arrived[RIM * q : RIM * q + RIM, :]

    kqs[:8, :] = halo[:, features:]
    kqs[8:, :] = kq_ref[...].astype(F32)
    wkq = wkq_ref[...].astype(F32)
    for i in range(2 * GRP_DEV):
        cs = slice(i * STATE, (i + 1) * STATE)
        acc = jnp.broadcast_to(bkq_ref[:, cs].astype(F32), (SPAN, STATE))
        for tap in range(KERNEL):
            acc = acc + wkq[tap : tap + 1, cs] * kqs[8 - RIM + tap : 8 - RIM + tap + SPAN, cs]
        act = silu(acc)
        if i < GRP_DEV:
            keys_t[i] = jnp.transpose(act).astype(BF16)
        else:
            queries[i - GRP_DEV] = act.astype(BF16)

    def span_state(t, g):
        cs = pl.ds(pl.multiple_of(t * TILE, TILE), TILE)
        xs[:8, :] = halo[:, cs]
        xs[8:, :] = x_ref[:, cs].astype(F32)
        wx = wx_ref[:, cs].astype(F32)
        acc = jnp.broadcast_to(bx_ref[:, cs].astype(F32), (SPAN, TILE))
        for tap in range(KERNEL):
            acc = acc + wx[tap : tap + 1] * xs[8 - RIM + tap : 8 - RIM + tap + SPAN, :]
        v = silu(acc).astype(BF16)
        vals[:, cs] = v
        weighted = (dot(w2[...], hot[:, cs]) * v.astype(F32)).astype(BF16)
        return dot(keys_t[g], weighted)

    other = 1 - side

    def s_copy(k):
        return remote(s_send.at[k], s_recv.at[k], s_ssem.at[k], s_rsem.at[k], partner)

    def c_copy(k):
        return remote(c_send.at[k], c_recv.at[k], c_ssem.at[k], c_rsem.at[k], jnp.minimum(me + 2, peers - 2 + side))

    def e_copy(k):
        return remote(e_send.at[k], e_recv.at[k], e_ssem.at[k], e_rsem.at[k], partner)

    @pl.loop(0, half_tiles)
    def _(k):
        s_send[k] = span_state(other * half_tiles + k, other).astype(BF16)
        s_copy(k).start()

    @pl.loop(0, half_tiles)
    def _(k):
        s_own[k] = span_state(side * half_tiles + k, side)

    for g in range(GRP_DEV):
        scores[g] = dot(queries[g], keys_t[g])

    f_copy.wait_recv()
    rows = jnp.concatenate(
        [factor, f_recv[:1, :], jnp.concatenate([skip, skip], axis=1), jnp.zeros((13, 2 * HEAD_DEV), F32)], axis=0
    )
    rows2[...] = two_terms(rows)
    ssq[...] = jnp.zeros_like(ssq)

    def local_part(t, g, skip_row):
        cs = pl.ds(pl.multiple_of(t * TILE, TILE), TILE)
        rolled = pltpu.roll(cum2[...], HEAD_DEV - t * TILE_HEADS, 1)
        sc = scores[g]
        cut = mask[...]
        lane = lax.broadcasted_iota(jnp.int32, (SPAN, 2 * HEAD_SIZE), 1)
        v_all = vals[:, cs]
        parts = []
        for pair in range(TILE_HEADS // 2):
            mixes = []
            for i in range(2):
                n = 2 * pair + i
                gap = rolled[:, n : n + 1] - row_t[pl.ds(t * TILE_HEADS + n, 1), :] + cut
                mixes.append((sc * jnp.exp2(gap)).astype(BF16))
            v = v_all[:, pair * 2 * HEAD_SIZE : (pair + 1) * 2 * HEAD_SIZE]
            vf = v.astype(F32)
            block = jnp.concatenate(
                [jnp.where(lane < HEAD_SIZE, vf, 0.0), jnp.where(lane < HEAD_SIZE, 0.0, vf)], axis=0
            ).astype(BF16)
            parts.append(dot(jnp.concatenate(mixes, axis=1), block))
        inside = jnp.concatenate(parts, axis=1)
        gate = silu(gate_ref[:, cs].astype(F32))
        res[:, cs] = (inside + skip_row * v_all.astype(F32)) * gate
        mix_gate[:, cs] = dot(g2[...], hot[:, cs]) * gate

    def read_back(t, g, entering):
        cs = pl.ds(pl.multiple_of(t * TILE, TILE), TILE)
        gated = res[:, cs] + mix_gate[:, cs] * dot(queries[g], entering)
        res[:, cs] = gated
        sq = gated * gated
        ssq[g] += sq[:, :STATE] + sq[:, STATE:]

    def finish(g):
        mean = jnp.sum(ssq[g], axis=1, keepdims=True) * (1.0 / (half_tiles * TILE))
        scale = lax.rsqrt(mean + 1e-05)

        @pl.loop(0, half_tiles)
        def _(k):
            cs = pl.ds(pl.multiple_of((g * half_tiles + k) * TILE, TILE), TILE)
            out_ref[:, cs] = ((res[:, cs] * scale) * gain_ref[:, cs]).astype(BF16)

    @pl.loop(0, half_tiles)
    def _(k):
        t = side * half_tiles + k
        u = other * half_tiles + k
        cs = pl.ds(pl.multiple_of(t * TILE, TILE), TILE)
        us = pl.ds(pl.multiple_of(u * TILE, TILE), TILE)
        own_rows = dot(rows2[...], hot[:, cs])
        other_rows = dot(rows2[...], hot[:, us])
        f_own = own_rows[0:1]
        f_oth = own_rows[1:2]
        s_copy(k).wait_recv()

        @pl.when(row > 0)
        def _():
            c_copy(k).wait_recv()

        @pl.when(side == 0)
        def _():
            mid = f_own * c_recv[k].astype(F32) + s_own[k]
            c_send[k] = (f_oth * mid + s_recv[k].astype(F32)).astype(BF16)
            e_send[k] = mid.astype(BF16)
            e_own[k] = c_recv[k]

        @pl.when(side == 1)
        def _():
            mid = f_oth * c_recv[k].astype(F32) + s_recv[k].astype(F32)
            c_send[k] = (f_own * mid + s_own[k]).astype(BF16)
            e_send[k] = c_recv[k]
            e_own[k] = mid.astype(BF16)

        @pl.when(row < last_row)
        def _():
            c_copy(k).start()

        e_copy(k).start()
        local_part(t, side, own_rows[2:3])
        read_back(t, side, e_own[k])
        local_part(u, other, other_rows[2:3])

    finish(side)

    @pl.loop(0, half_tiles)
    def _(k):
        e_copy(k).wait_recv()
        read_back(other * half_tiles + k, other, e_recv[k])

    finish(other)

    @pl.when(me < peers - 1)
    def _():
        halo_copy.wait_send()

    f_copy.wait_send()

    @pl.loop(0, half_tiles)
    def _(k):
        s_copy(k).wait_send()
        e_copy(k).wait_send()

        @pl.when(row < last_row)
        def _():
            c_copy(k).wait_send()


def shards(
    mixer_input,
    keys_queries,
    gate_input,
    step_raw,
    mixer_weight,
    mixer_bias,
    keyquery_weight,
    keyquery_bias,
    step_bias,
    decay_log,
    skip_gain,
    norm_gain,
    resets,
):
    length, features = mixer_input.shape
    peers = lax.axis_size("seq")
    pair_width = 2 * keys_queries.shape[2]
    tiles = features // TILE
    half = tiles // 2
    split = (features + pair_width) // 4
    vmem = pl.BlockSpec(memory_space=pltpu.VMEM)
    dma = pltpu.SemaphoreType.DMA
    chunk = (half, STATE, TILE)
    return pl.pallas_call(
        functools.partial(kernel, peers, tiles, split),
        out_shape=jax.ShapeDtypeStruct((length, features), BF16),
        in_specs=[vmem] * 12 + [pl.BlockSpec(memory_space=pltpu.SMEM)],
        out_specs=vmem,
        scratch_shapes=[
            pltpu.VMEM((16, split), BF16),
            pltpu.VMEM((16, split), BF16),
            pltpu.VMEM((8, features + pair_width), F32),
            pltpu.VMEM((SPAN + 8, TILE), F32),
            pltpu.VMEM((SPAN + 8, pair_width), F32),
            pltpu.VMEM((SPAN, features), BF16),
            pltpu.VMEM((SPAN, features), BF16),
            pltpu.VMEM((SPAN, 2 * HEAD_DEV), BF16),
            pltpu.VMEM((SPAN, 2 * HEAD_DEV), BF16),
            pltpu.VMEM((SPAN, 2 * HEAD_DEV), F32),
            pltpu.VMEM((2 * HEAD_DEV, SPAN), F32),
            pltpu.VMEM((GRP_DEV, STATE, SPAN), BF16),
            pltpu.VMEM((GRP_DEV, SPAN, STATE), BF16),
            pltpu.VMEM((GRP_DEV, SPAN, SPAN), F32),
            pltpu.VMEM((SPAN, SPAN), F32),
            pltpu.VMEM((16, 2 * HEAD_DEV), BF16),
            pltpu.VMEM((8, 2 * HEAD_DEV), F32),
            pltpu.VMEM((8, 2 * HEAD_DEV), F32),
            pltpu.VMEM(chunk, BF16),
            pltpu.VMEM(chunk, BF16),
            pltpu.VMEM(chunk, F32),
            pltpu.VMEM(chunk, BF16),
            pltpu.VMEM(chunk, BF16),
            pltpu.VMEM(chunk, BF16),
            pltpu.VMEM(chunk, BF16),
            pltpu.VMEM(chunk, BF16),
            pltpu.VMEM((SPAN, features), F32),
            pltpu.VMEM((SPAN, features), F32),
            pltpu.VMEM((GRP_DEV, SPAN, STATE), F32),
            dma((2,)),
            dma((2,)),
            dma((half,)),
            dma((half,)),
            dma((half,)),
            dma((half,)),
            dma((half,)),
            dma((half,)),
        ],
        compiler_params=pltpu.CompilerParams(
            collective_id=0, has_side_effects=True, vmem_limit_bytes=40 * 1024 * 1024
        ),
    )(
        mixer_input,
        keys_queries.reshape(length, pair_width),
        gate_input,
        step_raw,
        mixer_weight,
        mixer_bias.reshape(1, features),
        keyquery_weight.reshape(KERNEL, pair_width),
        keyquery_bias.reshape(1, pair_width),
        step_bias.reshape(1, HEAD_DEV),
        decay_log.reshape(1, HEAD_DEV),
        skip_gain.reshape(1, HEAD_DEV),
        norm_gain.reshape(1, features),
        resets,
    )


def solution(mesh):
    in_specs = (
        P(("groups", "seq"), "head"),
        P(("groups", "seq"), None, "head"),
        P(("groups", "seq"), "head"),
        P(("groups", "seq"), "head"),
        P(None, "head"),
        P("head"),
        P(None, None, "head"),
        P(None, "head"),
        P("head"),
        P("head"),
        P("head"),
        P("head"),
        P(("groups", "seq")),
    )
    out_specs = P(("groups", "seq"), "head")
    return jax.shard_map(shards, mesh=mesh, in_specs=in_specs, out_specs=out_specs, check_vma=False)
```

```python
import functools

import jax
import jax.numpy as jnp
from jax import lax
from jax.experimental import pallas as pl
from jax.experimental.pallas import tpu as pltpu
from jax.sharding import PartitionSpec as P

HEAD_DEV = 64
GRP_DEV = 2
HEAD_SIZE = 64
STATE = 128
SPAN = 128
KERNEL = 4
RIM = KERNEL - 1
TILE = 256
TILE_HEADS = TILE // HEAD_SIZE
LOG2E = 1.4426950408889634
F32 = jnp.float32
BF16 = jnp.bfloat16
MESH = pl.DeviceIdType.MESH


def silu(x):
    half = 0.5 * x
    return half * jnp.tanh(half) + half


def two_terms(x):
    lane = lax.broadcasted_iota(jnp.int32, x.shape, 1)
    lead = x.astype(BF16).astype(F32)
    return jnp.where(lane < HEAD_DEV, lead, x - lead).astype(BF16)


def dot(a, b):
    return jnp.dot(a, b, preferred_element_type=F32)


def kernel(
    peers, tiles, split,
    x_hbm, kq_hbm, gate_hbm, step_hbm, wx_hbm, bx_hbm, wkq_hbm, bkq_hbm,
    sbias_hbm, dlog_hbm, skip_hbm, gain_hbm, resets_ref,
    out_ref,
    x_ref, kq_ref, gate_ref, step_ref, wx_ref, bx_ref, wkq_ref, bkq_ref, sbias_ref, dlog_ref, skip_ref, gain_ref,
    tail_ref, in_sem, bx,
    halo_send, halo_recv, halo, xs, kqs, vals, hot, w2, g2, cum2, row_t, keys_t, queries, scores, mask,
    rows2, f_send, f_recv, s_send, s_recv, s_own, c_recv, c_send, e_send, e_recv, e_own, res, mix_gate, ssq,
    one_send, one_recv, s_ssem, s_rsem, c_ssem, c_rsem, e_ssem, e_rsem,
):
    me = lax.axis_index("seq")
    side = lax.rem(me, 2)
    row = me // 2
    partner = me + 1 - 2 * side
    last_row = peers // 2 - 1
    features = tiles * TILE
    half_tiles = tiles // 2
    quarter = split

    sources = (x_hbm.at[SPAN - 16 :], kq_hbm, step_hbm, sbias_hbm, dlog_hbm, skip_hbm, wkq_hbm, bkq_hbm, x_hbm,
               wx_hbm, bx_hbm, gate_hbm, gain_hbm)
    places = (tail_ref, kq_ref, step_ref, sbias_ref, dlog_ref, skip_ref, wkq_ref, bkq_ref, x_ref,
              wx_ref, bx_ref, gate_ref, gain_ref)
    loads = [pltpu.make_async_copy(src, dst, in_sem.at[i]) for i, (src, dst) in enumerate(zip(sources, places))]
    for load in loads:
        load.start()
    barrier = pltpu.get_barrier_semaphore()
    for away in (-2, -1, 1, 2):
        @pl.when((me + away >= 0) & (me + away < peers))
        def _(away=away):
            pl.semaphore_signal(barrier, inc=1, device_id={"seq": me + away}, device_id_type=MESH)
    loads[0].wait()
    loads[1].wait()
    pairs = kq_ref[...].astype(F32)
    pairs = jnp.concatenate([pairs[:, 0, :], pairs[:, 1, :]], axis=1)
    kqs[8:, :] = pairs
    rim = jnp.concatenate([tail_ref[...].astype(F32)[16 - RIM :], pairs[SPAN - RIM :]], axis=1)
    rim_parts = [rim[:, q * quarter : (q + 1) * quarter] for q in range(4)]
    halo_send[...] = jnp.concatenate(rim_parts + [jnp.zeros((4, quarter), F32)], axis=0).astype(BF16)
    pl.semaphore_wait(barrier, jnp.minimum(me, 2) + jnp.minimum(peers - 1 - me, 2))

    def remote(src, dst, ssem, rsem, target):
        return pltpu.make_async_remote_copy(
            src_ref=src, dst_ref=dst, send_sem=ssem, recv_sem=rsem, device_id={"seq": target}, device_id_type=MESH
        )

    halo_copy = remote(halo_send, halo_recv, one_send.at[0], one_recv.at[0], jnp.minimum(me + 1, peers - 1))

    @pl.when(me < peers - 1)
    def _():
        halo_copy.start()

    @pl.when(me == 0)
    def _():
        halo_recv[...] = jnp.zeros_like(halo_recv)

    survive = 1.0 - resets_ref[0].astype(F32)

    for load in loads[2:6]:
        load.wait()
    raw = step_ref[...].astype(F32)
    both = jnp.transpose(jnp.concatenate([raw, raw], axis=0))
    sbias = sbias_ref[...]
    dlog = dlog_ref[...]
    skip = skip_ref[...]
    logit = both + jnp.concatenate([sbias, sbias], axis=1)
    step = jnp.maximum(logit, 0.0) + jnp.log1p(jnp.exp(-jnp.abs(logit)))
    rate = (-LOG2E * jnp.exp(jnp.concatenate([dlog, dlog], axis=1))) * step
    t_idx = lax.broadcasted_iota(jnp.int32, (SPAN, SPAN), 0)
    s_idx = lax.broadcasted_iota(jnp.int32, (SPAN, SPAN), 1)
    lower = (t_idx >= s_idx).astype(F32)
    cum = jnp.dot(lower, rate, precision=lax.Precision.HIGHEST, preferred_element_type=F32)
    cum2[...] = cum
    end = cum[SPAN - 1 :, :]
    w2[...] = two_terms(jnp.exp2(end - cum) * step)
    g2[...] = two_terms(jnp.exp2(cum) * survive)
    factor = jnp.exp2(end) * survive
    f_send[...] = jnp.broadcast_to(factor, f_send.shape)
    f_copy = remote(f_send, f_recv, one_send.at[1], one_recv.at[1], partner)
    f_copy.start()
    row_t[...] = jnp.transpose(cum - jnp.log2(step))
    mask[...] = jnp.where(t_idx >= s_idx, 0.0, -1e30)

    @pl.loop(0, tiles)
    def _(t):
        r = lax.broadcasted_iota(jnp.int32, (SPAN, TILE), 0)
        c = lax.broadcasted_iota(jnp.int32, (SPAN, TILE), 1)
        hot[:, pl.ds(pl.multiple_of(t * TILE, TILE), TILE)] = (
            ((r & (HEAD_DEV - 1)) == t * TILE_HEADS + (c >> 6)).astype(F32).astype(BF16)
        )

    @pl.when(row == 0)
    def _():
        @pl.loop(0, half_tiles)
        def _(k):
            c_recv[k] = jnp.zeros((STATE, TILE), BF16)

    @pl.when(me > 0)
    def _():
        halo_copy.wait_recv()

    arrived = halo_recv[...].astype(F32) * survive
    for q in range(4):
        halo[8 - RIM :, q * quarter : (q + 1) * quarter] = arrived[RIM * q : RIM * q + RIM, :]

    kqs[:8, :] = halo[:, features:]
    for load in loads[6:11]:
        load.wait()
    wkq = wkq_ref[...].astype(F32)
    wkq = jnp.concatenate([wkq[:, 0, :], wkq[:, 1, :]], axis=1)
    bkq = bkq_ref[...].astype(F32)
    bkq = jnp.concatenate([bkq[:1], bkq[1:]], axis=1)
    bx[...] = bx_ref[...].astype(F32).reshape(1, features)
    for i in range(2 * GRP_DEV):
        cs = slice(i * STATE, (i + 1) * STATE)
        acc = jnp.broadcast_to(bkq[:, cs], (SPAN, STATE))
        for tap in range(KERNEL):
            acc = acc + wkq[tap : tap + 1, cs] * kqs[8 - RIM + tap : 8 - RIM + tap + SPAN, cs]
        act = silu(acc)
        if i < GRP_DEV:
            keys_t[i] = jnp.transpose(act).astype(BF16)
        else:
            queries[i - GRP_DEV] = act.astype(BF16)

    def span_state(t, g):
        cs = pl.ds(pl.multiple_of(t * TILE, TILE), TILE)
        xs[:8, :] = halo[:, cs]
        xs[8:, :] = x_ref[:, cs].astype(F32)
        wx = wx_ref[:, cs].astype(F32)
        acc = jnp.broadcast_to(bx[:, cs], (SPAN, TILE))
        for tap in range(KERNEL):
            acc = acc + wx[tap : tap + 1] * xs[8 - RIM + tap : 8 - RIM + tap + SPAN, :]
        v = silu(acc).astype(BF16)
        vals[:, cs] = v
        weighted = (dot(w2[...], hot[:, cs]) * v.astype(F32)).astype(BF16)
        return dot(keys_t[g], weighted)

    other = 1 - side

    def s_copy(k):
        return remote(s_send.at[k], s_recv.at[k], s_ssem.at[k], s_rsem.at[k], partner)

    def c_copy(k):
        return remote(c_send.at[k], c_recv.at[k], c_ssem.at[k], c_rsem.at[k], jnp.minimum(me + 2, peers - 2 + side))

    def e_copy(k):
        return remote(e_send.at[k], e_recv.at[k], e_ssem.at[k], e_rsem.at[k], partner)

    @pl.loop(0, half_tiles)
    def _(k):
        s_send[k] = span_state(other * half_tiles + k, other).astype(BF16)
        s_copy(k).start()

    @pl.loop(0, half_tiles)
    def _(k):
        s_own[k] = span_state(side * half_tiles + k, side)

    loads[11].wait()
    loads[12].wait()
    for g in range(GRP_DEV):
        scores[g] = dot(queries[g], keys_t[g])

    f_copy.wait_recv()
    rows = jnp.concatenate(
        [factor, f_recv[:1, :], jnp.concatenate([skip, skip], axis=1), jnp.zeros((13, 2 * HEAD_DEV), F32)], axis=0
    )
    rows2[...] = two_terms(rows)
    ssq[...] = jnp.zeros_like(ssq)

    def local_part(t, g, skip_row):
        cs = pl.ds(pl.multiple_of(t * TILE, TILE), TILE)
        rolled = pltpu.roll(cum2[...], HEAD_DEV - t * TILE_HEADS, 1)
        sc = scores[g]
        cut = mask[...]
        lane = lax.broadcasted_iota(jnp.int32, (SPAN, 2 * HEAD_SIZE), 1)
        v_all = vals[:, cs]
        parts = []
        for pair in range(TILE_HEADS // 2):
            mixes = []
            for i in range(2):
                n = 2 * pair + i
                gap = rolled[:, n : n + 1] - row_t[pl.ds(t * TILE_HEADS + n, 1), :] + cut
                mixes.append((sc * jnp.exp2(gap)).astype(BF16))
            v = v_all[:, pair * 2 * HEAD_SIZE : (pair + 1) * 2 * HEAD_SIZE]
            vf = v.astype(F32)
            block = jnp.concatenate(
                [jnp.where(lane < HEAD_SIZE, vf, 0.0), jnp.where(lane < HEAD_SIZE, 0.0, vf)], axis=0
            ).astype(BF16)
            parts.append(dot(jnp.concatenate(mixes, axis=1), block))
        inside = jnp.concatenate(parts, axis=1)
        gate = silu(gate_ref[:, cs].astype(F32))
        res[:, cs] = (inside + skip_row * v_all.astype(F32)) * gate
        mix_gate[:, cs] = dot(g2[...], hot[:, cs]) * gate

    def read_back(t, g, entering):
        cs = pl.ds(pl.multiple_of(t * TILE, TILE), TILE)
        gated = res[:, cs] + mix_gate[:, cs] * dot(queries[g], entering)
        res[:, cs] = gated
        sq = gated * gated
        ssq[g] += sq[:, :STATE] + sq[:, STATE:]

    def finish(g):
        mean = jnp.sum(ssq[g], axis=1, keepdims=True) * (1.0 / (half_tiles * TILE))
        scale = lax.rsqrt(mean + 1e-05)

        @pl.loop(0, half_tiles)
        def _(k):
            cs = pl.ds(pl.multiple_of((g * half_tiles + k) * TILE, TILE), TILE)
            out_ref[:, cs] = ((res[:, cs] * scale) * gain_ref[:, cs]).astype(BF16)

    @pl.loop(0, half_tiles)
    def _(k):
        t = side * half_tiles + k
        u = other * half_tiles + k
        cs = pl.ds(pl.multiple_of(t * TILE, TILE), TILE)
        us = pl.ds(pl.multiple_of(u * TILE, TILE), TILE)
        own_rows = dot(rows2[...], hot[:, cs])
        other_rows = dot(rows2[...], hot[:, us])
        f_own = own_rows[0:1]
        f_oth = own_rows[1:2]
        s_copy(k).wait_recv()

        @pl.when(row > 0)
        def _():
            c_copy(k).wait_recv()

        @pl.when(side == 0)
        def _():
            mid = f_own * c_recv[k].astype(F32) + s_own[k]
            c_send[k] = (f_oth * mid + s_recv[k].astype(F32)).astype(BF16)
            e_send[k] = mid.astype(BF16)
            e_own[k] = c_recv[k]

        @pl.when(side == 1)
        def _():
            mid = f_oth * c_recv[k].astype(F32) + s_recv[k].astype(F32)
            c_send[k] = (f_own * mid + s_own[k]).astype(BF16)
            e_send[k] = c_recv[k]
            e_own[k] = mid.astype(BF16)

        @pl.when(row < last_row)
        def _():
            c_copy(k).start()

        e_copy(k).start()
        local_part(t, side, own_rows[2:3])
        read_back(t, side, e_own[k])
        local_part(u, other, other_rows[2:3])

    finish(side)

    @pl.loop(0, half_tiles)
    def _(k):
        e_copy(k).wait_recv()
        read_back(other * half_tiles + k, other, e_recv[k])

    finish(other)

    @pl.when(me < peers - 1)
    def _():
        halo_copy.wait_send()

    f_copy.wait_send()

    @pl.loop(0, half_tiles)
    def _(k):
        s_copy(k).wait_send()
        e_copy(k).wait_send()

        @pl.when(row < last_row)
        def _():
            c_copy(k).wait_send()


def shards(
    mixer_input,
    keys_queries,
    gate_input,
    step_raw,
    mixer_weight,
    mixer_bias,
    keyquery_weight,
    keyquery_bias,
    step_bias,
    decay_log,
    skip_gain,
    norm_gain,
    resets,
):
    length, features = mixer_input.shape
    peers = lax.axis_size("seq")
    pair_width = 2 * keys_queries.shape[2]
    tiles = features // TILE
    half = tiles // 2
    split = (features + pair_width) // 4
    vmem = pl.BlockSpec(memory_space=pltpu.VMEM)
    hbm = pl.BlockSpec(memory_space=pltpu.HBM)
    operands = (
        mixer_input,
        keys_queries,
        gate_input,
        step_raw.T,
        mixer_weight,
        mixer_bias,
        keyquery_weight,
        keyquery_bias,
        step_bias.reshape(1, HEAD_DEV),
        decay_log.reshape(1, HEAD_DEV),
        skip_gain.reshape(1, HEAD_DEV),
        norm_gain.reshape(1, features),
    )
    dma = pltpu.SemaphoreType.DMA
    chunk = (half, STATE, TILE)
    return pl.pallas_call(
        functools.partial(kernel, peers, tiles, split),
        out_shape=jax.ShapeDtypeStruct((length, features), BF16),
        in_specs=[hbm] * 12 + [pl.BlockSpec(memory_space=pltpu.SMEM)],
        out_specs=vmem,
        scratch_shapes=[pltpu.VMEM(a.shape, a.dtype) for a in operands]
        + [
            pltpu.VMEM((16, features), BF16),
            dma((13,)),
            pltpu.VMEM((1, features), F32),
            pltpu.VMEM((16, split), BF16),
            pltpu.VMEM((16, split), BF16),
            pltpu.VMEM((8, features + pair_width), F32),
            pltpu.VMEM((SPAN + 8, TILE), F32),
            pltpu.VMEM((SPAN + 8, pair_width), F32),
            pltpu.VMEM((SPAN, features), BF16),
            pltpu.VMEM((SPAN, features), BF16),
            pltpu.VMEM((SPAN, 2 * HEAD_DEV), BF16),
            pltpu.VMEM((SPAN, 2 * HEAD_DEV), BF16),
            pltpu.VMEM((SPAN, 2 * HEAD_DEV), F32),
            pltpu.VMEM((2 * HEAD_DEV, SPAN), F32),
            pltpu.VMEM((GRP_DEV, STATE, SPAN), BF16),
            pltpu.VMEM((GRP_DEV, SPAN, STATE), BF16),
            pltpu.VMEM((GRP_DEV, SPAN, SPAN), F32),
            pltpu.VMEM((SPAN, SPAN), F32),
            pltpu.VMEM((16, 2 * HEAD_DEV), BF16),
            pltpu.VMEM((8, 2 * HEAD_DEV), F32),
            pltpu.VMEM((8, 2 * HEAD_DEV), F32),
            pltpu.VMEM(chunk, BF16),
            pltpu.VMEM(chunk, BF16),
            pltpu.VMEM(chunk, F32),
            pltpu.VMEM(chunk, BF16),
            pltpu.VMEM(chunk, BF16),
            pltpu.VMEM(chunk, BF16),
            pltpu.VMEM(chunk, BF16),
            pltpu.VMEM(chunk, BF16),
            pltpu.VMEM((SPAN, features), F32),
            pltpu.VMEM((SPAN, features), F32),
            pltpu.VMEM((GRP_DEV, SPAN, STATE), F32),
            dma((2,)),
            dma((2,)),
            dma((half,)),
            dma((half,)),
            dma((half,)),
            dma((half,)),
            dma((half,)),
            dma((half,)),
        ],
        compiler_params=pltpu.CompilerParams(
            collective_id=0, has_side_effects=True, vmem_limit_bytes=60 * 1024 * 1024
        ),
    )(*operands, resets)


def solution(mesh):
    in_specs = (
        P(("groups", "seq"), "head"),
        P(("groups", "seq"), None, "head"),
        P(("groups", "seq"), "head"),
        P(("groups", "seq"), "head"),
        P(None, "head"),
        P("head"),
        P(None, None, "head"),
        P(None, "head"),
        P("head"),
        P("head"),
        P("head"),
        P("head"),
        P(("groups", "seq")),
    )
    out_specs = P(("groups", "seq"), "head")
    return jax.shard_map(shards, mesh=mesh, in_specs=in_specs, out_specs=out_specs, check_vma=False)
```

```python
import functools

import jax
import jax.numpy as jnp
from jax import lax
from jax.experimental import pallas as pl
from jax.experimental.pallas import tpu as pltpu
from jax.sharding import PartitionSpec as P

HEAD_DEV = 64
GRP_DEV = 2
HEAD_SIZE = 64
STATE = 128
SPAN = 128
KERNEL = 4
RIM = KERNEL - 1
TILE = 256
TILE_HEADS = TILE // HEAD_SIZE
LOG2E = 1.4426950408889634
F32 = jnp.float32
BF16 = jnp.bfloat16
MESH = pl.DeviceIdType.MESH


def silu(x):
    half = 0.5 * x
    return half * jnp.tanh(half) + half


def two_terms(x):
    lane = lax.broadcasted_iota(jnp.int32, x.shape, 1)
    lead = x.astype(BF16).astype(F32)
    return jnp.where(lane < HEAD_DEV, lead, x - lead).astype(BF16)


def dot(a, b):
    return jnp.dot(a, b, preferred_element_type=F32)


def kernel(
    peers, tiles, split,
    x_hbm, kq_hbm, gate_hbm, step_hbm, wx_hbm, bx_hbm, wkq_hbm, bkq_hbm,
    sbias_hbm, dlog_hbm, skip_hbm, resets_ref,
    out_ref,
    x_ref, kq_ref, gate_ref, step_ref, wx_ref, bx_ref, wkq_ref, bkq_ref, sbias_ref, dlog_ref, skip_ref,
    tail_ref, in_sem, bx, out_sem,
    halo_send, halo_recv, halo, xs, kqs, vals, hot, w2, g2, cum2, row_t, keys_t, queries, scores, mask,
    rows2, f_send, f_recv, s_send, s_recv, s_own, c_recv, c_send, e_send, e_recv, e_own, res, mix_gate, ssq,
    one_send, one_recv, s_ssem, s_rsem, c_ssem, c_rsem, e_ssem, e_rsem,
):
    me = lax.axis_index("seq")
    side = lax.rem(me, 2)
    row = me // 2
    partner = me + 1 - 2 * side
    last_row = peers // 2 - 1
    features = tiles * TILE
    half_tiles = tiles // 2
    quarter = split

    sources = (x_hbm.at[SPAN - 16 :], kq_hbm, step_hbm, sbias_hbm, dlog_hbm, skip_hbm, wkq_hbm, bkq_hbm, x_hbm,
               wx_hbm, bx_hbm, gate_hbm)
    places = (tail_ref, kq_ref, step_ref, sbias_ref, dlog_ref, skip_ref, wkq_ref, bkq_ref, x_ref,
              wx_ref, bx_ref, gate_ref)
    loads = [pltpu.make_async_copy(src, dst, in_sem.at[i]) for i, (src, dst) in enumerate(zip(sources, places))]
    for load in loads:
        load.start()
    barrier = pltpu.get_barrier_semaphore()
    for away in (-2, -1, 1, 2):
        @pl.when((me + away >= 0) & (me + away < peers))
        def _(away=away):
            pl.semaphore_signal(barrier, inc=1, device_id={"seq": me + away}, device_id_type=MESH)
    @pl.loop(0, tiles)
    def _(t):
        r = lax.broadcasted_iota(jnp.int32, (SPAN, TILE), 0)
        c = lax.broadcasted_iota(jnp.int32, (SPAN, TILE), 1)
        hot[:, pl.ds(pl.multiple_of(t * TILE, TILE), TILE)] = (
            ((r & (HEAD_DEV - 1)) == t * TILE_HEADS + (c >> 6)).astype(F32).astype(BF16)
        )

    loads[0].wait()
    loads[1].wait()
    pairs = kq_ref[...].astype(F32)
    pairs = jnp.concatenate([pairs[:, 0, :], pairs[:, 1, :]], axis=1)
    kqs[8:, :] = pairs
    rim = jnp.concatenate([tail_ref[...].astype(F32)[16 - RIM :], pairs[SPAN - RIM :]], axis=1)
    rim_parts = [rim[:, q * quarter : (q + 1) * quarter] for q in range(4)]
    halo_send[...] = jnp.concatenate(rim_parts + [jnp.zeros((4, quarter), F32)], axis=0).astype(BF16)
    pl.semaphore_wait(barrier, jnp.minimum(me, 2) + jnp.minimum(peers - 1 - me, 2))

    def remote(src, dst, ssem, rsem, target):
        return pltpu.make_async_remote_copy(
            src_ref=src, dst_ref=dst, send_sem=ssem, recv_sem=rsem, device_id={"seq": target}, device_id_type=MESH
        )

    halo_copy = remote(halo_send, halo_recv, one_send.at[0], one_recv.at[0], jnp.minimum(me + 1, peers - 1))

    @pl.when(me < peers - 1)
    def _():
        halo_copy.start()

    @pl.when(me == 0)
    def _():
        halo_recv[...] = jnp.zeros_like(halo_recv)

    survive = 1.0 - resets_ref[0].astype(F32)

    for load in loads[2:6]:
        load.wait()
    raw = step_ref[...].astype(F32)
    both = jnp.transpose(jnp.concatenate([raw, raw], axis=0))
    sbias = sbias_ref[...]
    dlog = dlog_ref[...]
    skip = skip_ref[...]
    logit = both + jnp.concatenate([sbias, sbias], axis=1)
    step = jnp.maximum(logit, 0.0) + jnp.log1p(jnp.exp(-jnp.abs(logit)))
    rate = (-LOG2E * jnp.exp(jnp.concatenate([dlog, dlog], axis=1))) * step
    t_idx = lax.broadcasted_iota(jnp.int32, (SPAN, SPAN), 0)
    s_idx = lax.broadcasted_iota(jnp.int32, (SPAN, SPAN), 1)
    lower = (t_idx >= s_idx).astype(F32)
    cum = jnp.dot(lower, rate, precision=lax.Precision.HIGHEST, preferred_element_type=F32)
    cum2[...] = cum
    end = cum[SPAN - 1 :, :]
    w2[...] = two_terms(jnp.exp2(end - cum) * step)
    g2[...] = two_terms(jnp.exp2(cum) * survive)
    factor = jnp.exp2(end) * survive
    f_send[...] = jnp.broadcast_to(factor, f_send.shape)
    f_copy = remote(f_send, f_recv, one_send.at[1], one_recv.at[1], partner)
    f_copy.start()
    row_t[...] = jnp.transpose(cum - jnp.log2(step))
    mask[...] = jnp.where(t_idx >= s_idx, 0.0, -1e30)

    @pl.when(me > 0)
    def _():
        halo_copy.wait_recv()

    arrived = halo_recv[...].astype(F32) * survive
    for q in range(4):
        halo[8 - RIM :, q * quarter : (q + 1) * quarter] = arrived[RIM * q : RIM * q + RIM, :]

    kqs[:8, :] = halo[:, features:]
    for load in loads[6:11]:
        load.wait()
    wkq = wkq_ref[...].astype(F32)
    wkq = jnp.concatenate([wkq[:, 0, :], wkq[:, 1, :]], axis=1)
    bkq = bkq_ref[...].astype(F32)
    bkq = jnp.concatenate([bkq[:1], bkq[1:]], axis=1)
    bx[...] = bx_ref[...].astype(F32).reshape(1, features)
    for i in range(2 * GRP_DEV):
        cs = slice(i * STATE, (i + 1) * STATE)
        acc = jnp.broadcast_to(bkq[:, cs], (SPAN, STATE))
        for tap in range(KERNEL):
            acc = acc + wkq[tap : tap + 1, cs] * kqs[8 - RIM + tap : 8 - RIM + tap + SPAN, cs]
        act = silu(acc)
        if i < GRP_DEV:
            keys_t[i] = jnp.transpose(act).astype(BF16)
        else:
            queries[i - GRP_DEV] = act.astype(BF16)

    def span_state(t, g):
        cs = pl.ds(pl.multiple_of(t * TILE, TILE), TILE)
        xs[:8, :] = halo[:, cs]
        xs[8:, :] = x_ref[:, cs].astype(F32)
        wx = wx_ref[:, cs].astype(F32)
        acc = jnp.broadcast_to(bx[:, cs], (SPAN, TILE))
        for tap in range(KERNEL):
            acc = acc + wx[tap : tap + 1] * xs[8 - RIM + tap : 8 - RIM + tap + SPAN, :]
        v = silu(acc).astype(BF16)
        vals[:, cs] = v
        weighted = (dot(w2[...], hot[:, cs]) * v.astype(F32)).astype(BF16)
        return dot(keys_t[g], weighted)

    other = 1 - side

    def s_copy(k):
        return remote(s_send.at[k], s_recv.at[k], s_ssem.at[k], s_rsem.at[k], partner)

    def c_copy(k):
        return remote(c_send.at[k], c_recv.at[k], c_ssem.at[k], c_rsem.at[k], jnp.minimum(me + 2, peers - 2 + side))

    def e_copy(k):
        return remote(e_send.at[k], e_recv.at[k], e_ssem.at[k], e_rsem.at[k], partner)

    @pl.loop(0, half_tiles)
    def _(k):
        s_send[k] = span_state(other * half_tiles + k, other).astype(BF16)
        s_copy(k).start()

    @pl.loop(0, half_tiles)
    def _(k):
        s_own[k] = span_state(side * half_tiles + k, side)

    loads[11].wait()
    @pl.when(row == 0)
    def _():
        @pl.loop(0, half_tiles)
        def _(k):
            c_recv[k] = jnp.zeros((STATE, TILE), BF16)

    for g in range(GRP_DEV):
        scores[g] = dot(queries[g], keys_t[g])

    f_copy.wait_recv()
    rows = jnp.concatenate(
        [factor, f_recv[:1, :], jnp.concatenate([skip, skip], axis=1), jnp.zeros((13, 2 * HEAD_DEV), F32)], axis=0
    )
    rows2[...] = two_terms(rows)
    ssq[...] = jnp.zeros_like(ssq)

    def local_part(t, g, skip_row):
        cs = pl.ds(pl.multiple_of(t * TILE, TILE), TILE)
        rolled = pltpu.roll(cum2[...], HEAD_DEV - t * TILE_HEADS, 1)
        sc = scores[g]
        cut = mask[...]
        lane = lax.broadcasted_iota(jnp.int32, (SPAN, 2 * HEAD_SIZE), 1)
        v_all = vals[:, cs]
        parts = []
        for pair in range(TILE_HEADS // 2):
            mixes = []
            for i in range(2):
                n = 2 * pair + i
                gap = rolled[:, n : n + 1] - row_t[pl.ds(t * TILE_HEADS + n, 1), :] + cut
                mixes.append((sc * jnp.exp2(gap)).astype(BF16))
            v = v_all[:, pair * 2 * HEAD_SIZE : (pair + 1) * 2 * HEAD_SIZE]
            vf = v.astype(F32)
            block = jnp.concatenate(
                [jnp.where(lane < HEAD_SIZE, vf, 0.0), jnp.where(lane < HEAD_SIZE, 0.0, vf)], axis=0
            ).astype(BF16)
            parts.append(dot(jnp.concatenate(mixes, axis=1), block))
        inside = jnp.concatenate(parts, axis=1)
        gate = silu(gate_ref[:, cs].astype(F32))
        res[:, cs] = (inside + skip_row * v_all.astype(F32)) * gate
        mix_gate[:, cs] = dot(g2[...], hot[:, cs]) * gate

    def read_back(t, g, entering):
        cs = pl.ds(pl.multiple_of(t * TILE, TILE), TILE)
        gated = res[:, cs] + mix_gate[:, cs] * dot(queries[g], entering)
        res[:, cs] = gated
        sq = gated * gated
        ssq[g] += sq[:, :STATE] + sq[:, STATE:]

    def out_copy(g, k):
        cs = pl.ds(pl.multiple_of((g * half_tiles + k) * TILE, TILE), TILE)
        return pltpu.make_async_copy(res.at[:, cs], out_ref.at[:, cs], out_sem.at[g, k])

    def finish(g):
        mean = jnp.sum(ssq[g], axis=1, keepdims=True) * (1.0 / (half_tiles * TILE))
        scale = lax.rsqrt(mean + 1e-05)

        @pl.loop(0, half_tiles)
        def _(k):
            cs = pl.ds(pl.multiple_of((g * half_tiles + k) * TILE, TILE), TILE)
            res[:, cs] = res[:, cs] * scale
            out_copy(g, k).start()

    def local_step(k):
        t = side * half_tiles + k
        u = other * half_tiles + k
        skips = [dot(rows2[...], hot[:, pl.ds(pl.multiple_of(n * TILE, TILE), TILE)])[2:3] for n in (t, u)]
        local_part(t, side, skips[0])
        local_part(u, other, skips[1])

    @pl.loop(0, half_tiles)
    def _(k):
        t = side * half_tiles + k
        cs = pl.ds(pl.multiple_of(t * TILE, TILE), TILE)
        own_rows = dot(rows2[...], hot[:, cs])
        f_own = own_rows[0:1]
        f_oth = own_rows[1:2]
        s_copy(k).wait_recv()

        @pl.when(row > 0)
        def _():
            c_copy(k).wait_recv()

        @pl.when(side == 0)
        def _():
            mid = f_own * c_recv[k].astype(F32) + s_own[k]
            c_send[k] = (f_oth * mid + s_recv[k].astype(F32)).astype(BF16)
            e_send[k] = mid.astype(BF16)
            e_own[k] = c_recv[k]

        @pl.when(side == 1)
        def _():
            mid = f_oth * c_recv[k].astype(F32) + s_recv[k].astype(F32)
            c_send[k] = (f_own * mid + s_own[k]).astype(BF16)
            e_send[k] = c_recv[k]
            e_own[k] = mid.astype(BF16)

        @pl.when(row < last_row)
        def _():
            c_copy(k).start()

        e_copy(k).start()
        local_step(k)
        read_back(t, side, e_own[k])

    finish(side)

    @pl.loop(0, half_tiles)
    def _(k):
        e_copy(k).wait_recv()
        read_back(other * half_tiles + k, other, e_recv[k])

    finish(other)

    @pl.loop(0, half_tiles)
    def _(k):
        out_copy(side, k).wait()
        out_copy(other, k).wait()

    @pl.when(me < peers - 1)
    def _():
        halo_copy.wait_send()

    f_copy.wait_send()

    @pl.loop(0, half_tiles)
    def _(k):
        s_copy(k).wait_send()
        e_copy(k).wait_send()

        @pl.when(row < last_row)
        def _():
            c_copy(k).wait_send()


def shards(
    mixer_input,
    keys_queries,
    gate_input,
    step_raw,
    mixer_weight,
    mixer_bias,
    keyquery_weight,
    keyquery_bias,
    step_bias,
    decay_log,
    skip_gain,
    norm_gain,
    resets,
):
    length, features = mixer_input.shape
    peers = lax.axis_size("seq")
    pair_width = 2 * keys_queries.shape[2]
    tiles = features // TILE
    half = tiles // 2
    split = (features + pair_width) // 4
    hbm = pl.BlockSpec(memory_space=pltpu.HBM)
    operands = (
        mixer_input,
        keys_queries,
        gate_input,
        step_raw.T,
        mixer_weight,
        mixer_bias,
        keyquery_weight,
        keyquery_bias,
        step_bias.reshape(1, HEAD_DEV),
        decay_log.reshape(1, HEAD_DEV),
        skip_gain.reshape(1, HEAD_DEV),
    )
    dma = pltpu.SemaphoreType.DMA
    chunk = (half, STATE, TILE)
    normed = pl.pallas_call(
        functools.partial(kernel, peers, tiles, split),
        out_shape=jax.ShapeDtypeStruct((length, features), F32),
        in_specs=[hbm] * 11 + [pl.BlockSpec(memory_space=pltpu.SMEM)],
        out_specs=hbm,
        scratch_shapes=[pltpu.VMEM(a.shape, a.dtype) for a in operands]
        + [
            pltpu.VMEM((16, features), BF16),
            dma((12,)),
            pltpu.VMEM((1, features), F32),
            dma((2, half)),
            pltpu.VMEM((16, split), BF16),
            pltpu.VMEM((16, split), BF16),
            pltpu.VMEM((8, features + pair_width), F32),
            pltpu.VMEM((SPAN + 8, TILE), F32),
            pltpu.VMEM((SPAN + 8, pair_width), F32),
            pltpu.VMEM((SPAN, features), BF16),
            pltpu.VMEM((SPAN, features), BF16),
            pltpu.VMEM((SPAN, 2 * HEAD_DEV), BF16),
            pltpu.VMEM((SPAN, 2 * HEAD_DEV), BF16),
            pltpu.VMEM((SPAN, 2 * HEAD_DEV), F32),
            pltpu.VMEM((2 * HEAD_DEV, SPAN), F32),
            pltpu.VMEM((GRP_DEV, STATE, SPAN), BF16),
            pltpu.VMEM((GRP_DEV, SPAN, STATE), BF16),
            pltpu.VMEM((GRP_DEV, SPAN, SPAN), F32),
            pltpu.VMEM((SPAN, SPAN), F32),
            pltpu.VMEM((16, 2 * HEAD_DEV), BF16),
            pltpu.VMEM((8, 2 * HEAD_DEV), F32),
            pltpu.VMEM((8, 2 * HEAD_DEV), F32),
            pltpu.VMEM(chunk, BF16),
            pltpu.VMEM(chunk, BF16),
            pltpu.VMEM(chunk, F32),
            pltpu.VMEM(chunk, BF16),
            pltpu.VMEM(chunk, BF16),
            pltpu.VMEM(chunk, BF16),
            pltpu.VMEM(chunk, BF16),
            pltpu.VMEM(chunk, BF16),
            pltpu.VMEM((SPAN, features), F32),
            pltpu.VMEM((SPAN, features), F32),
            pltpu.VMEM((GRP_DEV, SPAN, STATE), F32),
            dma((2,)),
            dma((2,)),
            dma((half,)),
            dma((half,)),
            dma((half,)),
            dma((half,)),
            dma((half,)),
            dma((half,)),
        ],
        compiler_params=pltpu.CompilerParams(
            collective_id=0, has_side_effects=True, vmem_limit_bytes=60 * 1024 * 1024
        ),
    )(*operands, resets)
    return (normed * norm_gain).astype(BF16)


def solution(mesh):
    in_specs = (
        P(("groups", "seq"), "head"),
        P(("groups", "seq"), None, "head"),
        P(("groups", "seq"), "head"),
        P(("groups", "seq"), "head"),
        P(None, "head"),
        P("head"),
        P(None, None, "head"),
        P(None, "head"),
        P("head"),
        P("head"),
        P("head"),
        P("head"),
        P(("groups", "seq")),
    )
    out_specs = P(("groups", "seq"), "head")
    return jax.shard_map(shards, mesh=mesh, in_specs=in_specs, out_specs=out_specs, check_vma=False)
```

```python
import functools

import jax
import jax.numpy as jnp
from jax import lax
from jax.experimental import pallas as pl
from jax.experimental.pallas import tpu as pltpu
from jax.sharding import PartitionSpec as P

HEAD_DEV = 64
GRP_DEV = 2
HEAD_SIZE = 64
STATE = 128
SPAN = 128
KERNEL = 4
RIM = KERNEL - 1
TILE = 256
TILE_HEADS = TILE // HEAD_SIZE
LOG2E = 1.4426950408889634
F32 = jnp.float32
BF16 = jnp.bfloat16
MESH = pl.DeviceIdType.MESH


def silu(x):
    half = 0.5 * x
    return half * jnp.tanh(half) + half


def two_terms(x):
    lane = lax.broadcasted_iota(jnp.int32, x.shape, 1)
    lead = x.astype(BF16).astype(F32)
    return jnp.where(lane < HEAD_DEV, lead, x - lead).astype(BF16)


def dot(a, b):
    return jnp.dot(a, b, preferred_element_type=F32)


def kernel(
    peers, tiles, split,
    x_hbm, kq_hbm, gate_hbm, step_hbm, wx_hbm, bx_hbm, wkq_hbm, bkq_hbm,
    sbias_hbm, dlog_hbm, skip_hbm, gain_hbm, resets_ref,
    out_ref,
    x_ref, kq_ref, gate_ref, step_ref, wx_ref, bx_ref, wkq_ref, bkq_ref, sbias_ref, dlog_ref, skip_ref, gain_ref,
    tail_ref, in_sem, bx,
    halo_send, halo_recv, halo, xs, kqs, vals, hot, w2, g2, cum2, row_t, keys_t, queries, scores, mask,
    rows2, f_send, f_recv, s_send, s_recv, s_own, c_recv, c_send, e_send, e_recv, e_own, res, mix_gate, ssq,
    one_send, one_recv, s_ssem, s_rsem, c_ssem, c_rsem, e_ssem, e_rsem,
):
    me = lax.axis_index("seq")
    side = lax.rem(me, 2)
    row = me // 2
    partner = me + 1 - 2 * side
    last_row = peers // 2 - 1
    features = tiles * TILE
    half_tiles = tiles // 2
    quarter = split

    sources = (x_hbm.at[SPAN - 16 :], kq_hbm, step_hbm, sbias_hbm, dlog_hbm, skip_hbm, wkq_hbm, bkq_hbm, x_hbm,
               wx_hbm, bx_hbm, gate_hbm, gain_hbm)
    places = (tail_ref, kq_ref, step_ref, sbias_ref, dlog_ref, skip_ref, wkq_ref, bkq_ref, x_ref,
              wx_ref, bx_ref, gate_ref, gain_ref)
    loads = [pltpu.make_async_copy(src, dst, in_sem.at[i]) for i, (src, dst) in enumerate(zip(sources, places))]
    for load in loads:
        load.start()
    barrier = pltpu.get_barrier_semaphore()
    for away in (-2, -1, 1, 2):
        @pl.when((me + away >= 0) & (me + away < peers))
        def _(away=away):
            pl.semaphore_signal(barrier, inc=1, device_id={"seq": me + away}, device_id_type=MESH)
    loads[0].wait()
    loads[1].wait()
    last = kq_ref[SPAN - 8 :].astype(F32)
    last = jnp.concatenate([last[:, 0, :], last[:, 1, :]], axis=1)
    rim = jnp.concatenate([tail_ref[...].astype(F32)[16 - RIM :], last[8 - RIM :]], axis=1)
    rim_parts = [rim[:, q * quarter : (q + 1) * quarter] for q in range(4)]
    halo_send[...] = jnp.concatenate(rim_parts + [jnp.zeros((4, quarter), F32)], axis=0).astype(BF16)
    pl.semaphore_wait(barrier, jnp.minimum(me, 2) + jnp.minimum(peers - 1 - me, 2))

    def remote(src, dst, ssem, rsem, target):
        return pltpu.make_async_remote_copy(
            src_ref=src, dst_ref=dst, send_sem=ssem, recv_sem=rsem, device_id={"seq": target}, device_id_type=MESH
        )

    halo_copy = remote(halo_send, halo_recv, one_send.at[0], one_recv.at[0], jnp.minimum(me + 1, peers - 1))

    @pl.when(me < peers - 1)
    def _():
        halo_copy.start()

    @pl.when(me == 0)
    def _():
        halo_recv[...] = jnp.zeros_like(halo_recv)

    survive = 1.0 - resets_ref[0].astype(F32)

    pairs = kq_ref[...].astype(F32)
    kqs[8:, :] = jnp.concatenate([pairs[:, 0, :], pairs[:, 1, :]], axis=1)

    for load in loads[2:6]:
        load.wait()
    raw = step_ref[...].astype(F32)
    both = jnp.transpose(jnp.concatenate([raw, raw], axis=0))
    sbias = sbias_ref[...]
    dlog = dlog_ref[...]
    skip = skip_ref[...]
    logit = both + jnp.concatenate([sbias, sbias], axis=1)
    step = jnp.maximum(logit, 0.0) + jnp.log1p(jnp.exp(-jnp.abs(logit)))
    rate = (-LOG2E * jnp.exp(jnp.concatenate([dlog, dlog], axis=1))) * step
    t_idx = lax.broadcasted_iota(jnp.int32, (SPAN, SPAN), 0)
    s_idx = lax.broadcasted_iota(jnp.int32, (SPAN, SPAN), 1)
    lower = (t_idx >= s_idx).astype(F32)
    cum = jnp.dot(lower, rate, precision=lax.Precision.HIGHEST, preferred_element_type=F32)
    cum2[...] = cum
    end = cum[SPAN - 1 :, :]
    w2[...] = two_terms(jnp.exp2(end - cum) * step)
    g2[...] = two_terms(jnp.exp2(cum) * survive)
    factor = jnp.exp2(end) * survive
    f_send[...] = jnp.broadcast_to(factor, f_send.shape)
    f_copy = remote(f_send, f_recv, one_send.at[1], one_recv.at[1], partner)
    f_copy.start()
    row_t[...] = jnp.transpose(cum - jnp.log2(step))
    mask[...] = jnp.where(t_idx >= s_idx, 0.0, -1e30)

    @pl.loop(0, tiles)
    def _(t):
        r = lax.broadcasted_iota(jnp.int32, (SPAN, TILE), 0)
        c = lax.broadcasted_iota(jnp.int32, (SPAN, TILE), 1)
        hot[:, pl.ds(pl.multiple_of(t * TILE, TILE), TILE)] = (
            ((r & (HEAD_DEV - 1)) == t * TILE_HEADS + (c >> 6)).astype(F32).astype(BF16)
        )

    @pl.when(row == 0)
    def _():
        @pl.loop(0, half_tiles)
        def _(k):
            c_recv[k] = jnp.zeros((STATE, TILE), BF16)

    @pl.when(me > 0)
    def _():
        halo_copy.wait_recv()

    arrived = halo_recv[...].astype(F32) * survive
    for q in range(4):
        halo[8 - RIM :, q * quarter : (q + 1) * quarter] = arrived[RIM * q : RIM * q + RIM, :]

    kqs[:8, :] = halo[:, features:]
    for load in loads[6:11]:
        load.wait()
    wkq = wkq_ref[...].astype(F32)
    wkq = jnp.concatenate([wkq[:, 0, :], wkq[:, 1, :]], axis=1)
    bkq = bkq_ref[...].astype(F32)
    bkq = jnp.concatenate([bkq[:1], bkq[1:]], axis=1)
    bx[...] = bx_ref[...].astype(F32).reshape(1, features)
    for i in range(2 * GRP_DEV):
        cs = slice(i * STATE, (i + 1) * STATE)
        acc = jnp.broadcast_to(bkq[:, cs], (SPAN, STATE))
        for tap in range(KERNEL):
            acc = acc + wkq[tap : tap + 1, cs] * kqs[8 - RIM + tap : 8 - RIM + tap + SPAN, cs]
        act = silu(acc)
        if i < GRP_DEV:
            keys_t[i] = jnp.transpose(act).astype(BF16)
        else:
            queries[i - GRP_DEV] = act.astype(BF16)

    def span_state(t, g):
        cs = pl.ds(pl.multiple_of(t * TILE, TILE), TILE)
        xs[:8, :] = halo[:, cs]
        xs[8:, :] = x_ref[:, cs].astype(F32)
        wx = wx_ref[:, cs].astype(F32)
        acc = jnp.broadcast_to(bx[:, cs], (SPAN, TILE))
        for tap in range(KERNEL):
            acc = acc + wx[tap : tap + 1] * xs[8 - RIM + tap : 8 - RIM + tap + SPAN, :]
        v = silu(acc).astype(BF16)
        vals[:, cs] = v
        weighted = (dot(w2[...], hot[:, cs]) * v.astype(F32)).astype(BF16)
        return dot(keys_t[g], weighted)

    other = 1 - side

    def s_copy(k):
        return remote(s_send.at[k], s_recv.at[k], s_ssem.at[k], s_rsem.at[k], partner)

    def c_copy(k):
        return remote(c_send.at[k], c_recv.at[k], c_ssem.at[k], c_rsem.at[k], jnp.minimum(me + 2, peers - 2 + side))

    def e_copy(k):
        return remote(e_send.at[k], e_recv.at[k], e_ssem.at[k], e_rsem.at[k], partner)

    @pl.loop(0, half_tiles)
    def _(k):
        s_send[k] = span_state(other * half_tiles + k, other).astype(BF16)
        s_copy(k).start()

    @pl.loop(0, half_tiles)
    def _(k):
        s_own[k] = span_state(side * half_tiles + k, side)

    loads[11].wait()
    loads[12].wait()
    for g in range(GRP_DEV):
        scores[g] = dot(queries[g], keys_t[g])

    f_copy.wait_recv()
    rows = jnp.concatenate(
        [factor, f_recv[:1, :], jnp.concatenate([skip, skip], axis=1), jnp.zeros((13, 2 * HEAD_DEV), F32)], axis=0
    )
    rows2[...] = two_terms(rows)
    ssq[...] = jnp.zeros_like(ssq)

    def local_part(t, g, skip_row):
        cs = pl.ds(pl.multiple_of(t * TILE, TILE), TILE)
        rolled = pltpu.roll(cum2[...], HEAD_DEV - t * TILE_HEADS, 1)
        sc = scores[g]
        cut = mask[...]
        lane = lax.broadcasted_iota(jnp.int32, (SPAN, 2 * HEAD_SIZE), 1)
        v_all = vals[:, cs]
        parts = []
        for pair in range(TILE_HEADS // 2):
            mixes = []
            for i in range(2):
                n = 2 * pair + i
                gap = rolled[:, n : n + 1] - row_t[pl.ds(t * TILE_HEADS + n, 1), :] + cut
                mixes.append((sc * jnp.exp2(gap)).astype(BF16))
            v = v_all[:, pair * 2 * HEAD_SIZE : (pair + 1) * 2 * HEAD_SIZE]
            vf = v.astype(F32)
            block = jnp.concatenate(
                [jnp.where(lane < HEAD_SIZE, vf, 0.0), jnp.where(lane < HEAD_SIZE, 0.0, vf)], axis=0
            ).astype(BF16)
            parts.append(dot(jnp.concatenate(mixes, axis=1), block))
        inside = jnp.concatenate(parts, axis=1)
        gate = silu(gate_ref[:, cs].astype(F32))
        res[:, cs] = (inside + skip_row * v_all.astype(F32)) * gate
        mix_gate[:, cs] = dot(g2[...], hot[:, cs]) * gate

    def read_back(t, g, entering):
        cs = pl.ds(pl.multiple_of(t * TILE, TILE), TILE)
        gated = res[:, cs] + mix_gate[:, cs] * dot(queries[g], entering)
        res[:, cs] = gated
        sq = gated * gated
        ssq[g] += sq[:, :STATE] + sq[:, STATE:]

    def finish(g):
        mean = jnp.sum(ssq[g], axis=1, keepdims=True) * (1.0 / (half_tiles * TILE))
        scale = lax.rsqrt(mean + 1e-05)

        @pl.loop(0, half_tiles)
        def _(k):
            cs = pl.ds(pl.multiple_of((g * half_tiles + k) * TILE, TILE), TILE)
            out_ref[:, cs] = ((res[:, cs] * scale) * gain_ref[:, cs]).astype(BF16)

    @pl.loop(0, half_tiles)
    def _(k):
        t = side * half_tiles + k
        u = other * half_tiles + k
        cs = pl.ds(pl.multiple_of(t * TILE, TILE), TILE)
        us = pl.ds(pl.multiple_of(u * TILE, TILE), TILE)
        own_rows = dot(rows2[...], hot[:, cs])
        other_rows = dot(rows2[...], hot[:, us])
        f_own = own_rows[0:1]
        f_oth = own_rows[1:2]
        s_copy(k).wait_recv()

        @pl.when(row > 0)
        def _():
            c_copy(k).wait_recv()

        @pl.when(side == 0)
        def _():
            mid = f_own * c_recv[k].astype(F32) + s_own[k]
            c_send[k] = (f_oth * mid + s_recv[k].astype(F32)).astype(BF16)
            e_send[k] = mid.astype(BF16)
            e_own[k] = c_recv[k]

        @pl.when(side == 1)
        def _():
            mid = f_oth * c_recv[k].astype(F32) + s_recv[k].astype(F32)
            c_send[k] = (f_own * mid + s_own[k]).astype(BF16)
            e_send[k] = c_recv[k]
            e_own[k] = mid.astype(BF16)

        @pl.when(row < last_row)
        def _():
            c_copy(k).start()

        e_copy(k).start()
        local_part(t, side, own_rows[2:3])
        read_back(t, side, e_own[k])
        local_part(u, other, other_rows[2:3])

    finish(side)

    @pl.loop(0, half_tiles)
    def _(k):
        e_copy(k).wait_recv()
        read_back(other * half_tiles + k, other, e_recv[k])

    finish(other)

    @pl.when(me < peers - 1)
    def _():
        halo_copy.wait_send()

    f_copy.wait_send()

    @pl.loop(0, half_tiles)
    def _(k):
        s_copy(k).wait_send()
        e_copy(k).wait_send()

        @pl.when(row < last_row)
        def _():
            c_copy(k).wait_send()


def shards(
    mixer_input,
    keys_queries,
    gate_input,
    step_raw,
    mixer_weight,
    mixer_bias,
    keyquery_weight,
    keyquery_bias,
    step_bias,
    decay_log,
    skip_gain,
    norm_gain,
    resets,
):
    length, features = mixer_input.shape
    peers = lax.axis_size("seq")
    pair_width = 2 * keys_queries.shape[2]
    tiles = features // TILE
    half = tiles // 2
    split = (features + pair_width) // 4
    vmem = pl.BlockSpec(memory_space=pltpu.VMEM)
    hbm = pl.BlockSpec(memory_space=pltpu.HBM)
    operands = (
        mixer_input,
        keys_queries,
        gate_input,
        step_raw.T,
        mixer_weight,
        mixer_bias,
        keyquery_weight,
        keyquery_bias,
        step_bias.reshape(1, HEAD_DEV),
        decay_log.reshape(1, HEAD_DEV),
        skip_gain.reshape(1, HEAD_DEV),
        norm_gain.reshape(1, features),
    )
    dma = pltpu.SemaphoreType.DMA
    chunk = (half, STATE, TILE)
    return pl.pallas_call(
        functools.partial(kernel, peers, tiles, split),
        out_shape=jax.ShapeDtypeStruct((length, features), BF16),
        in_specs=[hbm] * 12 + [pl.BlockSpec(memory_space=pltpu.SMEM)],
        out_specs=vmem,
        scratch_shapes=[pltpu.VMEM(a.shape, a.dtype) for a in operands]
        + [
            pltpu.VMEM((16, features), BF16),
            dma((13,)),
            pltpu.VMEM((1, features), F32),
            pltpu.VMEM((16, split), BF16),
            pltpu.VMEM((16, split), BF16),
            pltpu.VMEM((8, features + pair_width), F32),
            pltpu.VMEM((SPAN + 8, TILE), F32),
            pltpu.VMEM((SPAN + 8, pair_width), F32),
            pltpu.VMEM((SPAN, features), BF16),
            pltpu.VMEM((SPAN, features), BF16),
            pltpu.VMEM((SPAN, 2 * HEAD_DEV), BF16),
            pltpu.VMEM((SPAN, 2 * HEAD_DEV), BF16),
            pltpu.VMEM((SPAN, 2 * HEAD_DEV), F32),
            pltpu.VMEM((2 * HEAD_DEV, SPAN), F32),
            pltpu.VMEM((GRP_DEV, STATE, SPAN), BF16),
            pltpu.VMEM((GRP_DEV, SPAN, STATE), BF16),
            pltpu.VMEM((GRP_DEV, SPAN, SPAN), F32),
            pltpu.VMEM((SPAN, SPAN), F32),
            pltpu.VMEM((16, 2 * HEAD_DEV), BF16),
            pltpu.VMEM((8, 2 * HEAD_DEV), F32),
            pltpu.VMEM((8, 2 * HEAD_DEV), F32),
            pltpu.VMEM(chunk, BF16),
            pltpu.VMEM(chunk, BF16),
            pltpu.VMEM(chunk, F32),
            pltpu.VMEM(chunk, BF16),
            pltpu.VMEM(chunk, BF16),
            pltpu.VMEM(chunk, BF16),
            pltpu.VMEM(chunk, BF16),
            pltpu.VMEM(chunk, BF16),
            pltpu.VMEM((SPAN, features), F32),
            pltpu.VMEM((SPAN, features), F32),
            pltpu.VMEM((GRP_DEV, SPAN, STATE), F32),
            dma((2,)),
            dma((2,)),
            dma((half,)),
            dma((half,)),
            dma((half,)),
            dma((half,)),
            dma((half,)),
            dma((half,)),
        ],
        compiler_params=pltpu.CompilerParams(
            collective_id=0, has_side_effects=True, vmem_limit_bytes=60 * 1024 * 1024
        ),
    )(*operands, resets)


def solution(mesh):
    in_specs = (
        P(("groups", "seq"), "head"),
        P(("groups", "seq"), None, "head"),
        P(("groups", "seq"), "head"),
        P(("groups", "seq"), "head"),
        P(None, "head"),
        P("head"),
        P(None, None, "head"),
        P(None, "head"),
        P("head"),
        P("head"),
        P("head"),
        P("head"),
        P(("groups", "seq")),
    )
    out_specs = P(("groups", "seq"), "head")
    return jax.shard_map(shards, mesh=mesh, in_specs=in_specs, out_specs=out_specs, check_vma=False)
```

```python
import functools

import jax
import jax.numpy as jnp
from jax import lax
from jax.experimental import pallas as pl
from jax.experimental.pallas import tpu as pltpu
from jax.sharding import PartitionSpec as P

HEAD_DEV = 64
GRP_DEV = 2
HEAD_SIZE = 64
STATE = 128
SPAN = 128
KERNEL = 4
RIM = KERNEL - 1
TILE = 256
TILE_HEADS = TILE // HEAD_SIZE
LOG2E = 1.4426950408889634
F32 = jnp.float32
BF16 = jnp.bfloat16
MESH = pl.DeviceIdType.MESH


def silu(x):
    half = 0.5 * x
    return half * jnp.tanh(half) + half


def two_terms(x):
    lane = lax.broadcasted_iota(jnp.int32, x.shape, 1)
    lead = x.astype(BF16).astype(F32)
    return jnp.where(lane < HEAD_DEV, lead, x - lead).astype(BF16)


def dot(a, b):
    return jnp.dot(a, b, preferred_element_type=F32)


def kernel(
    peers, tiles, split,
    x_hbm, kq_hbm, gate_hbm, step_hbm, wx_hbm, bx_hbm, wkq_hbm, bkq_hbm,
    sbias_hbm, dlog_hbm, skip_hbm, gain_hbm, resets_ref,
    out_ref,
    x_ref, kq_ref, gate_ref, step_ref, wx_ref, bx_ref, wkq_ref, bkq_ref, sbias_ref, dlog_ref, skip_ref, gain_ref,
    tail_ref, in_sem, bx,
    halo_send, halo_recv, halo, xs, kqs, vals, hot, w2, g2, cum2, row_t, keys_t, queries, scores, mask,
    rows2, f_send, f_recv, s_send, s_recv, s_own, c_recv, c_send, e_send, e_recv, e_own, res, mix_gate, ssq,
    one_send, one_recv, s_ssem, s_rsem, c_ssem, c_rsem, e_ssem, e_rsem,
):
    me = lax.axis_index("seq")
    side = lax.rem(me, 2)
    row = me // 2
    partner = me + 1 - 2 * side
    last_row = peers // 2 - 1
    features = tiles * TILE
    half_tiles = tiles // 2
    quarter = split

    sources = (x_hbm.at[SPAN - 16 :], kq_hbm, step_hbm, sbias_hbm, dlog_hbm, skip_hbm, wkq_hbm, bkq_hbm, x_hbm,
               wx_hbm, bx_hbm, gate_hbm, gain_hbm)
    places = (tail_ref, kq_ref, step_ref, sbias_ref, dlog_ref, skip_ref, wkq_ref, bkq_ref, x_ref,
              wx_ref, bx_ref, gate_ref, gain_ref)
    loads = [pltpu.make_async_copy(src, dst, in_sem.at[i]) for i, (src, dst) in enumerate(zip(sources, places))]
    for load in loads:
        load.start()
    barrier = pltpu.get_barrier_semaphore()
    for away in (-2, -1, 1, 2):
        @pl.when((me + away >= 0) & (me + away < peers))
        def _(away=away):
            pl.semaphore_signal(barrier, inc=1, device_id={"seq": me + away}, device_id_type=MESH)
    loads[0].wait()
    loads[1].wait()
    pairs = kq_ref[...].astype(F32)
    pairs = jnp.concatenate([pairs[:, 0, :], pairs[:, 1, :]], axis=1)
    kqs[8:, :] = pairs
    rim = jnp.concatenate([tail_ref[...].astype(F32)[16 - RIM :], pairs[SPAN - RIM :]], axis=1)
    rim_parts = [rim[:, q * quarter : (q + 1) * quarter] for q in range(4)]
    halo_send[...] = jnp.concatenate(rim_parts + [jnp.zeros((4, quarter), F32)], axis=0).astype(BF16)
    pl.semaphore_wait(barrier, jnp.minimum(me, 2) + jnp.minimum(peers - 1 - me, 2))

    def remote(src, dst, ssem, rsem, target):
        return pltpu.make_async_remote_copy(
            src_ref=src, dst_ref=dst, send_sem=ssem, recv_sem=rsem, device_id={"seq": target}, device_id_type=MESH
        )

    halo_copy = remote(halo_send, halo_recv, one_send.at[0], one_recv.at[0], jnp.minimum(me + 1, peers - 1))

    @pl.when(me < peers - 1)
    def _():
        halo_copy.start()

    @pl.when(me == 0)
    def _():
        halo_recv[...] = jnp.zeros_like(halo_recv)

    survive = 1.0 - resets_ref[0].astype(F32)

    for load in loads[2:6]:
        load.wait()
    raw = step_ref[...].astype(F32)
    both = jnp.transpose(jnp.concatenate([raw, raw], axis=0))
    sbias = sbias_ref[...]
    dlog = dlog_ref[...]
    skip = skip_ref[...]
    logit = both + jnp.concatenate([sbias, sbias], axis=1)
    step = jnp.maximum(logit, 0.0) + jnp.log1p(jnp.exp(-jnp.abs(logit)))
    rate = (-LOG2E * jnp.exp(jnp.concatenate([dlog, dlog], axis=1))) * step
    t_idx = lax.broadcasted_iota(jnp.int32, (SPAN, SPAN), 0)
    s_idx = lax.broadcasted_iota(jnp.int32, (SPAN, SPAN), 1)
    lower = (t_idx >= s_idx).astype(F32)
    cum = jnp.dot(lower, rate, precision=lax.Precision.HIGHEST, preferred_element_type=F32)
    cum2[...] = cum
    end = cum[SPAN - 1 :, :]
    w2[...] = two_terms(jnp.exp2(end - cum) * step)
    g2[...] = two_terms(jnp.exp2(cum) * survive)
    factor = jnp.exp2(end) * survive
    f_send[...] = jnp.broadcast_to(factor, f_send.shape)
    f_copy = remote(f_send, f_recv, one_send.at[1], one_recv.at[1], partner)
    f_copy.start()
    row_t[...] = jnp.transpose(cum - jnp.log2(step))
    mask[...] = jnp.where(t_idx >= s_idx, 0.0, -1e30)

    @pl.loop(0, tiles)
    def _(t):
        r = lax.broadcasted_iota(jnp.int32, (SPAN, TILE), 0)
        c = lax.broadcasted_iota(jnp.int32, (SPAN, TILE), 1)
        hot[:, pl.ds(pl.multiple_of(t * TILE, TILE), TILE)] = (
            ((r & (HEAD_DEV - 1)) == t * TILE_HEADS + (c >> 6)).astype(F32).astype(BF16)
        )

    @pl.when(row == 0)
    def _():
        @pl.loop(0, half_tiles)
        def _(k):
            c_recv[k] = jnp.zeros((STATE, TILE), BF16)

    @pl.when(me > 0)
    def _():
        halo_copy.wait_recv()

    arrived = halo_recv[...].astype(F32) * survive
    for q in range(4):
        halo[8 - RIM :, q * quarter : (q + 1) * quarter] = arrived[RIM * q : RIM * q + RIM, :]

    kqs[:8, :] = halo[:, features:]
    for load in loads[6:11]:
        load.wait()
    wkq = wkq_ref[...].astype(F32)
    wkq = jnp.concatenate([wkq[:, 0, :], wkq[:, 1, :]], axis=1)
    bkq = bkq_ref[...].astype(F32)
    bkq = jnp.concatenate([bkq[:1], bkq[1:]], axis=1)
    bx[...] = bx_ref[...].astype(F32).reshape(1, features)
    for i in range(2 * GRP_DEV):
        cs = slice(i * STATE, (i + 1) * STATE)
        acc = jnp.broadcast_to(bkq[:, cs], (SPAN, STATE))
        for tap in range(KERNEL):
            acc = acc + wkq[tap : tap + 1, cs] * kqs[8 - RIM + tap : 8 - RIM + tap + SPAN, cs]
        act = silu(acc)
        if i < GRP_DEV:
            keys_t[i] = jnp.transpose(act).astype(BF16)
        else:
            queries[i - GRP_DEV] = act.astype(BF16)

    def span_state(t, g):
        cs = pl.ds(pl.multiple_of(t * TILE, TILE), TILE)
        xs[:8, :] = halo[:, cs]
        xs[8:, :] = x_ref[:, cs].astype(F32)
        wx = wx_ref[:, cs].astype(F32)
        acc = jnp.broadcast_to(bx[:, cs], (SPAN, TILE))
        for tap in range(KERNEL):
            acc = acc + wx[tap : tap + 1] * xs[8 - RIM + tap : 8 - RIM + tap + SPAN, :]
        v = silu(acc).astype(BF16)
        vals[:, cs] = v
        weighted = (dot(w2[...], hot[:, cs]) * v.astype(F32)).astype(BF16)
        return dot(keys_t[g], weighted)

    other = 1 - side

    def s_copy(k):
        return remote(s_send.at[k], s_recv.at[k], s_ssem.at[k], s_rsem.at[k], partner)

    def c_copy(k):
        return remote(c_send.at[k], c_recv.at[k], c_ssem.at[k], c_rsem.at[k], jnp.minimum(me + 2, peers - 2 + side))

    def e_copy(k):
        return remote(e_send.at[k], e_recv.at[k], e_ssem.at[k], e_rsem.at[k], partner)

    @pl.loop(0, half_tiles)
    def _(k):
        s_send[k] = span_state(other * half_tiles + k, other).astype(BF16)
        s_copy(k).start()

    @pl.loop(0, half_tiles)
    def _(k):
        s_own[k] = span_state(side * half_tiles + k, side)

    loads[11].wait()
    loads[12].wait()
    for g in range(GRP_DEV):
        scores[g] = dot(queries[g], keys_t[g])

    f_copy.wait_recv()
    rows = jnp.concatenate(
        [factor, f_recv[:1, :], jnp.concatenate([skip, skip], axis=1), jnp.zeros((13, 2 * HEAD_DEV), F32)], axis=0
    )
    rows2[...] = two_terms(rows)
    ssq[...] = jnp.zeros_like(ssq)

    def local_part(t, g, skip_row):
        cs = pl.ds(pl.multiple_of(t * TILE, TILE), TILE)
        rolled = pltpu.roll(cum2[...], HEAD_DEV - t * TILE_HEADS, 1)
        sc = scores[g]
        cut = mask[...]
        lane = lax.broadcasted_iota(jnp.int32, (SPAN, 2 * HEAD_SIZE), 1)
        v_all = vals[:, cs]
        parts = []
        for pair in range(TILE_HEADS // 2):
            mixes = []
            for i in range(2):
                n = 2 * pair + i
                gap = rolled[:, n : n + 1] - row_t[pl.ds(t * TILE_HEADS + n, 1), :] + cut
                mixes.append((sc * jnp.exp2(gap)).astype(BF16))
            v = v_all[:, pair * 2 * HEAD_SIZE : (pair + 1) * 2 * HEAD_SIZE]
            vf = v.astype(F32)
            block = jnp.concatenate(
                [jnp.where(lane < HEAD_SIZE, vf, 0.0), jnp.where(lane < HEAD_SIZE, 0.0, vf)], axis=0
            ).astype(BF16)
            parts.append(dot(jnp.concatenate(mixes, axis=1), block))
        inside = jnp.concatenate(parts, axis=1)
        gate = silu(gate_ref[:, cs].astype(F32))
        res[:, cs] = (inside + skip_row * v_all.astype(F32)) * gate
        mix_gate[:, cs] = dot(g2[...], hot[:, cs]) * gate

    def read_back(t, g, entering):
        cs = pl.ds(pl.multiple_of(t * TILE, TILE), TILE)
        gated = res[:, cs] + mix_gate[:, cs] * dot(queries[g], entering)
        res[:, cs] = gated
        sq = gated * gated
        ssq[g] += sq[:, :STATE] + sq[:, STATE:]

    def finish(g):
        mean = jnp.sum(ssq[g], axis=1, keepdims=True) * (1.0 / (half_tiles * TILE))
        scale = lax.rsqrt(mean + 1e-05)

        @pl.loop(0, half_tiles)
        def _(k):
            cs = pl.ds(pl.multiple_of((g * half_tiles + k) * TILE, TILE), TILE)
            out_ref[:, cs] = ((res[:, cs] * scale) * gain_ref[:, cs]).astype(BF16)

    @pl.loop(0, half_tiles)
    def _(k):
        t = side * half_tiles + k
        u = other * half_tiles + k
        cs = pl.ds(pl.multiple_of(t * TILE, TILE), TILE)
        us = pl.ds(pl.multiple_of(u * TILE, TILE), TILE)
        own_rows = dot(rows2[...], hot[:, cs])
        other_rows = dot(rows2[...], hot[:, us])
        f_own = own_rows[0:1]
        f_oth = own_rows[1:2]
        s_copy(k).wait_recv()

        @pl.when(row > 0)
        def _():
            c_copy(k).wait_recv()

        @pl.when(side == 0)
        def _():
            mid = f_own * c_recv[k].astype(F32) + s_own[k]
            c_send[k] = (f_oth * mid + s_recv[k].astype(F32)).astype(BF16)
            e_send[k] = mid.astype(BF16)
            e_own[k] = c_recv[k]

        @pl.when(side == 1)
        def _():
            mid = f_oth * c_recv[k].astype(F32) + s_recv[k].astype(F32)
            c_send[k] = (f_own * mid + s_own[k]).astype(BF16)
            e_send[k] = c_recv[k]
            e_own[k] = mid.astype(BF16)

        @pl.when(row < last_row)
        def _():
            c_copy(k).start()

        e_copy(k).start()
        local_part(t, side, own_rows[2:3])
        read_back(t, side, e_own[k])
        local_part(u, other, other_rows[2:3])

        @pl.when((row == last_row) & (k >= 2))
        def _():
            e_copy(k - 2).wait_recv()
            read_back(u - 2, other, e_recv[k - 2])

    finish(side)

    @pl.loop((row // last_row) * (half_tiles - 2), half_tiles)
    def _(k):
        e_copy(k).wait_recv()
        read_back(other * half_tiles + k, other, e_recv[k])

    finish(other)

    @pl.when(me < peers - 1)
    def _():
        halo_copy.wait_send()

    f_copy.wait_send()

    @pl.loop(0, half_tiles)
    def _(k):
        s_copy(k).wait_send()
        e_copy(k).wait_send()

        @pl.when(row < last_row)
        def _():
            c_copy(k).wait_send()


def shards(
    mixer_input,
    keys_queries,
    gate_input,
    step_raw,
    mixer_weight,
    mixer_bias,
    keyquery_weight,
    keyquery_bias,
    step_bias,
    decay_log,
    skip_gain,
    norm_gain,
    resets,
):
    length, features = mixer_input.shape
    peers = lax.axis_size("seq")
    pair_width = 2 * keys_queries.shape[2]
    tiles = features // TILE
    half = tiles // 2
    split = (features + pair_width) // 4
    vmem = pl.BlockSpec(memory_space=pltpu.VMEM)
    hbm = pl.BlockSpec(memory_space=pltpu.HBM)
    operands = (
        mixer_input,
        keys_queries,
        gate_input,
        step_raw.T,
        mixer_weight,
        mixer_bias,
        keyquery_weight,
        keyquery_bias,
        step_bias.reshape(1, HEAD_DEV),
        decay_log.reshape(1, HEAD_DEV),
        skip_gain.reshape(1, HEAD_DEV),
        norm_gain.reshape(1, features),
    )
    dma = pltpu.SemaphoreType.DMA
    chunk = (half, STATE, TILE)
    return pl.pallas_call(
        functools.partial(kernel, peers, tiles, split),
        out_shape=jax.ShapeDtypeStruct((length, features), BF16),
        in_specs=[hbm] * 12 + [pl.BlockSpec(memory_space=pltpu.SMEM)],
        out_specs=vmem,
        scratch_shapes=[pltpu.VMEM(a.shape, a.dtype) for a in operands]
        + [
            pltpu.VMEM((16, features), BF16),
            dma((13,)),
            pltpu.VMEM((1, features), F32),
            pltpu.VMEM((16, split), BF16),
            pltpu.VMEM((16, split), BF16),
            pltpu.VMEM((8, features + pair_width), F32),
            pltpu.VMEM((SPAN + 8, TILE), F32),
            pltpu.VMEM((SPAN + 8, pair_width), F32),
            pltpu.VMEM((SPAN, features), BF16),
            pltpu.VMEM((SPAN, features), BF16),
            pltpu.VMEM((SPAN, 2 * HEAD_DEV), BF16),
            pltpu.VMEM((SPAN, 2 * HEAD_DEV), BF16),
            pltpu.VMEM((SPAN, 2 * HEAD_DEV), F32),
            pltpu.VMEM((2 * HEAD_DEV, SPAN), F32),
            pltpu.VMEM((GRP_DEV, STATE, SPAN), BF16),
            pltpu.VMEM((GRP_DEV, SPAN, STATE), BF16),
            pltpu.VMEM((GRP_DEV, SPAN, SPAN), F32),
            pltpu.VMEM((SPAN, SPAN), F32),
            pltpu.VMEM((16, 2 * HEAD_DEV), BF16),
            pltpu.VMEM((8, 2 * HEAD_DEV), F32),
            pltpu.VMEM((8, 2 * HEAD_DEV), F32),
            pltpu.VMEM(chunk, BF16),
            pltpu.VMEM(chunk, BF16),
            pltpu.VMEM(chunk, F32),
            pltpu.VMEM(chunk, BF16),
            pltpu.VMEM(chunk, BF16),
            pltpu.VMEM(chunk, BF16),
            pltpu.VMEM(chunk, BF16),
            pltpu.VMEM(chunk, BF16),
            pltpu.VMEM((SPAN, features), F32),
            pltpu.VMEM((SPAN, features), F32),
            pltpu.VMEM((GRP_DEV, SPAN, STATE), F32),
            dma((2,)),
            dma((2,)),
            dma((half,)),
            dma((half,)),
            dma((half,)),
            dma((half,)),
            dma((half,)),
            dma((half,)),
        ],
        compiler_params=pltpu.CompilerParams(
            collective_id=0, has_side_effects=True, vmem_limit_bytes=60 * 1024 * 1024
        ),
    )(*operands, resets)


def solution(mesh):
    in_specs = (
        P(("groups", "seq"), "head"),
        P(("groups", "seq"), None, "head"),
        P(("groups", "seq"), "head"),
        P(("groups", "seq"), "head"),
        P(None, "head"),
        P("head"),
        P(None, None, "head"),
        P(None, "head"),
        P("head"),
        P("head"),
        P("head"),
        P("head"),
        P(("groups", "seq")),
    )
    out_specs = P(("groups", "seq"), "head")
    return jax.shard_map(shards, mesh=mesh, in_specs=in_specs, out_specs=out_specs, check_vma=False)
```
